32 devices in a mesh: parts: 2 (over y), ep: 4 (over z), fs: 4 (over x, core).
Axes of the slice: x: 2, y: 2, z: 4, core: 2. Of those that a mesh axis runs over, the one named last changes fastest.
Arguments:
- hidden_states: bfloat16 [8, 512, 1152], P(('parts', 'fs'), 'ep'), parts along dimension 0, may hold values from -6 to 6
- expert_ids: int32 [8, 512, 2], P(('parts', 'fs'), 'ep'), parts along dimension 0, may hold values from 0 to 15, all different within a row; in each aligned block of 128 rows (0 to 127, 128 to 255, ..., all dimensions but the last counted through in order) at most 20 rows name the same one
- modulation: float32 [8, 3, 1152], P(('parts', 'fs')), parts along dimension 0, may hold values from -4 to 4
- router_weight: bfloat16 [1152, 16], replicated, may hold values from -0.1875 to 0.1875
- w_in: bfloat16 [32, 1152, 2304], P('ep', 'fs'), may hold values from -0.1875 to 0.1875
- b_in: float32 [32, 2304], P('ep'), may hold values from -3 to 3
- w_out: bfloat16 [32, 2304, 1152], P('ep', 'fs'), may hold values from -0.09375 to 0.09375
Outputs:
- layer_out: bfloat16 [8, 512, 1152], P(('parts', 'fs'), 'ep'), parts along dimension 0
The draws below stay inside these ranges and needn't reach their ends.
There are 2 independent parts, one for each index of `parts`. The reference program is written for one: setup_inputs(seed, part) draws one part's arguments, and reference() takes and returns one part's arrays. A program takes and returns all parts, laid end to end along the dimension named above; an argument that names none is the same for every part. Nothing has to cross between parts.
Inputs may be any that keep to these rules, and one draw needn't show every extreme that they name: `expert_ids`: the two ids of a token differ. In each aligned block of 128 tokens of an image, no expert is named by more than 20 tokens, a bound that some block reaches.
All inputs are finite; a program needn't handle non-finite values.
Results may differ from the reference program's by a relative error of at most 0.0046.
Values may be sent and summed in bfloat16 or wider, within the bound.
No kernel may reach another device: no remote copies, remote signals or barrier semaphores. Data moves between devices by JAX's collectives and lax.ppermute only.
A program may use at most 192 MiB of HBM per device.

```python
import math
import jax
import jax.numpy as jnp
import numpy as np
from jax import lax

D = 1152
FF = 4608
EXPERTS = 16
SPLIT = 2
TOK_DEV = 128
CAP = 20
FFU = 2304
UNITS = 32
LAT = 512
IMAGES = 4
N_EP = 4


def levels(rng, extent, pieces, smallest, largest):
    level, own = 1.0, jax.random.fold_in(rng, 6)
    for position, shards_of in pieces:
        draws = jnp.exp(jax.random.uniform(jax.random.fold_in(own, position), (shards_of,), jnp.float32, smallest / len(pieces), largest / len(pieces)))
        level = level * jnp.repeat(draws, extent[position] // shards_of).reshape([-1 if axis == position else 1 for axis in range(len(extent))])
    return level


def shared_out(own_key, own, number, rows, number_of, top, bound, slope):
    order = jax.random.permutation(own_key, number_of)
    crowded, usual = shares(number_of, rows * top, bound, slope, True), shares(number_of, rows * top, bound, slope, False)
    places = jnp.arange(number_of)

    def named(lengths, rotation):
        used = int((lengths > 0).sum())
        fixed = max(1, used // 4)
        shifted = fixed + (places - fixed + rotation * (used - fixed)) % max(1, number_of - fixed)
        return jnp.zeros((number_of,), jnp.int32).at[order[jnp.where(places < fixed, places, shifted)]].set(jnp.asarray(lengths, jnp.int32))

    lengths = jnp.where(number % 4 == 0, named(crowded, number // 4), named(usual, number - number // 4 - 1))
    mixed = jax.random.permutation(jax.random.fold_in(own, 3), number_of)
    source_of, sink = mixed[0:number_of // 2 * 2:2], mixed[1:number_of // 2 * 2:2]
    margin = jnp.minimum(lengths[source_of] - 1, bound - lengths[sink]) // 2
    margin = jnp.where((source_of == order[0]) | (sink == order[0]) | (lengths[sink] == 0), 0, jnp.maximum(margin, 0))
    shifted = jax.random.randint(jax.random.fold_in(own, 4), (number_of // 2,), 0, 1 << 20) % (margin + 1)
    lengths = lengths.at[source_of].add(-shifted).at[sink].add(shifted)
    labels = jnp.searchsorted(jnp.cumsum(lengths), jnp.arange(rows * top), side="right").astype(jnp.int32)
    listing = labels.reshape(top, rows).T
    listing = listing[jax.random.permutation(jax.random.fold_in(own, 1), rows)]
    rotation = jax.random.randint(jax.random.fold_in(own, 2), (rows, 1), 0, top)
    return jnp.take_along_axis(listing, (jnp.arange(top)[None, :] + rotation) % top, axis=1)


def shares(count, total, reach, slope, full):
    portions = [(1 << 20) // math.isqrt(standing ** slope) + 1 for standing in range(1, count + 1)]
    largest = reach if full else min(reach, max(-(-total // count), total * portions[0] // sum(portions)))
    least = 1 if total - largest >= count - 1 else 0
    given, spare = [largest] + [least] * (count - 1), total - largest - least * (count - 1)
    while spare > 0:
        free = [i for i in range(1, count) if given[i] < largest] or [i for i in range(1, count) if given[i] < reach]
        mass, remaining = sum([portions[i] for i in free]), spare
        for i in free:
            more = min(reach - given[i], max(1, remaining * portions[i] // mass), spare)
            given[i] = given[i] + more
            spare = spare - more
    return np.array(given)


def normal_values(rng, extent, width, limit, shards=(), kind=jnp.bfloat16):
    factor_of = levels(rng, extent, shards, -0.22, 0.18) if shards else 1.0
    array = jax.random.normal(rng, extent, jnp.float32) * width * factor_of
    return jnp.minimum(jnp.maximum(array, -limit), limit).astype(kind)


def setup_inputs(seed: int = 0, part: int = 0) -> dict:
    streams_of = jax.random.split(jax.random.key(seed), 8)
    part_splits = jax.random.split(jax.random.fold_in(streams_of[7], part), 8)
    hidden_states = normal_values(part_splits[0], (IMAGES, LAT, D), 1.0, 6.0, ((0, 4), (1, 4)))
    expert_ids_keys = jax.random.split(jax.random.fold_in(part_splits[1], 1), IMAGES * LAT // TOK_DEV)
    expert_ids_turns = jax.random.permutation(jax.random.fold_in(part_splits[1], 3), IMAGES * LAT // TOK_DEV)
    expert_ids = jax.vmap(lambda own, number: shared_out(jax.random.fold_in(part_splits[1], 2), own, number, TOK_DEV, EXPERTS, 2, CAP, 1))(expert_ids_keys, expert_ids_turns).reshape((IMAGES, LAT, 2))
    modulation = normal_values(part_splits[2], (IMAGES, 3, D), 0.6, 4.0, ((0, 4),), jnp.float32)
    router_weight = normal_values(streams_of[3], (D, EXPERTS), D ** -0.5, 0.1875)
    w_in = normal_values(streams_of[4], (UNITS, D, FFU), D ** -0.5, 0.1875, ((0, 4), (1, 4)))
    b_in = normal_values(streams_of[5], (UNITS, FFU), 0.5, 3.0, ((0, 4),), jnp.float32)
    w_out = normal_values(streams_of[6], (UNITS, FFU, D), FF ** -0.5, 0.09375, ((0, 4), (1, 4)))
    return dict(hidden_states=hidden_states, expert_ids=expert_ids, modulation=modulation, router_weight=router_weight, w_in=w_in, b_in=b_in, w_out=w_out)


norm_eps = 1e-06

def modulate(tokens, shift, scale):
    values = tokens.astype(jnp.float32)
    center = lax.optimization_barrier(jnp.mean(values, axis=-1, keepdims=True))
    spread = lax.optimization_barrier(jnp.mean(jnp.square(values - center), axis=-1, keepdims=True))
    normal = (values - center) * lax.rsqrt(spread + norm_eps)
    return (normal * (1.0 + scale) + shift).astype(jnp.bfloat16)

def slot_index(block_ids):
    flat_ids = block_ids.reshape(-1)
    one_hot = (flat_ids[:, None] == jnp.arange(EXPERTS, dtype=jnp.int32)[None, :]).astype(jnp.int32)
    earlier = jnp.cumsum(one_hot, axis=0, dtype=jnp.int32) - one_hot
    slots = lax.optimization_barrier(jnp.sum(earlier * one_hot, axis=1, dtype=jnp.int32))
    return (flat_ids * CAP + slots).astype(jnp.int32).reshape(block_ids.shape)

def dispatch_rows(normed, flat_index):
    targets = jnp.arange(EXPERTS * CAP, dtype=jnp.int32)
    select = lax.optimization_barrier(jnp.sum((flat_index[None, :, :] == targets[:, None, None]).astype(jnp.int32), axis=2, dtype=jnp.int32))
    return jnp.dot(select.astype(jnp.bfloat16), normed, preferred_element_type=jnp.float32).astype(jnp.bfloat16)

def combine(tokens, normed, gate_row, router_weight, block_ids, flat_index, expert_out):
    logits = jnp.dot(normed, router_weight, preferred_element_type=jnp.float32)
    picked = jnp.take_along_axis(logits, block_ids, axis=1)
    gap = picked[:, 0:1] - picked[:, 1:2]
    first = jnp.take(expert_out, flat_index[:, 0], axis=0).astype(jnp.float32)
    second = jnp.take(expert_out, flat_index[:, 1], axis=0).astype(jnp.float32)
    branch = jax.nn.sigmoid(gap) * first + jax.nn.sigmoid(-gap) * second
    return (tokens.astype(jnp.float32) + gate_row[None, :] * branch).astype(jnp.bfloat16)

def reference(hidden_states, expert_ids, modulation, router_weight, w_in, b_in, w_out):
    blocks_x = hidden_states.reshape(IMAGES, N_EP, TOK_DEV, D)
    blocks_ids = expert_ids.reshape(IMAGES, N_EP, TOK_DEV, 2)
    normed = modulate(blocks_x, modulation[:, None, None, 0, :], modulation[:, None, None, 1, :])
    flat_index = jax.vmap(jax.vmap(slot_index))(blocks_ids)
    outgoing = jax.vmap(jax.vmap(dispatch_rows))(normed, flat_index)
    per_expert = outgoing.reshape(IMAGES, N_EP, EXPERTS, CAP, D).transpose(2, 0, 1, 3, 4)
    per_expert = per_expert.reshape(EXPERTS, IMAGES * N_EP * CAP, D)

    def unit_work(packed):
        unit, first_w, first_b, second_w = packed
        rows = lax.dynamic_index_in_dim(per_expert, unit // SPLIT, 0, keepdims=False)
        pre = jnp.dot(rows, first_w, preferred_element_type=jnp.float32) + first_b[None, :]
        hidden = jax.nn.gelu(pre, approximate=True).astype(jnp.bfloat16)
        return jnp.dot(hidden, second_w, preferred_element_type=jnp.float32).astype(jnp.bfloat16)
    piece_out = lax.map(unit_work, (jnp.arange(UNITS, dtype=jnp.int32), w_in, b_in, w_out))
    expert_out = lax.optimization_barrier(jnp.sum(piece_out.astype(jnp.float32).reshape(EXPERTS, SPLIT, IMAGES, N_EP, CAP, D), axis=1))
    expert_out = expert_out.astype(jnp.bfloat16)
    expert_out = expert_out.transpose(1, 2, 0, 3, 4).reshape(IMAGES, N_EP, EXPERTS * CAP, D)
    inner = jax.vmap(combine, in_axes=(0, 0, None, None, 0, 0, 0))
    outer = jax.vmap(inner, in_axes=(0, 0, 0, None, 0, 0, 0))
    result = outer(blocks_x, normed, modulation[:, 2, :], router_weight, blocks_ids, flat_index, expert_out)
    return result.reshape(IMAGES, LAT, D)
```

```python
import functools

import jax
import jax.numpy as jnp
from jax import lax
from jax.experimental import pallas as pl
from jax.experimental.pallas import tpu as pltpu
from jax.sharding import PartitionSpec as P

EXPERTS = 16
SPLIT = 2
CAP = 20


norm_eps = 1e-06


def swapped(block, axis, distance):
    count = lax.axis_size(axis)
    route = []
    for low in range(count):
        high = low | 1 << distance
        if high != low and high < count:
            route += [(low, high), (high, low)]
    return lax.ppermute(block, axis, route)


def modulate(tokens, shift, scale):
    values = tokens.astype(jnp.float32)
    center = jnp.mean(values, axis=-1, keepdims=True)
    spread = jnp.mean(jnp.square(values - center), axis=-1, keepdims=True)
    normal = (values - center) * lax.rsqrt(spread + norm_eps)
    return (normal * (1.0 + scale) + shift).astype(jnp.bfloat16)


def slot_index(block_ids):
    flat_ids = block_ids.reshape(-1)
    one_hot = (flat_ids[:, None] == jnp.arange(EXPERTS, dtype=jnp.int32)[None, :]).astype(jnp.int32)
    earlier = jnp.cumsum(one_hot, axis=0, dtype=jnp.int32) - one_hot
    slots = jnp.sum(earlier * one_hot, axis=1, dtype=jnp.int32)
    return (flat_ids * CAP + slots).reshape(block_ids.shape)


def dispatch_rows(normed, flat_index):
    targets = jnp.arange(EXPERTS * CAP, dtype=jnp.int32)
    select = jnp.sum(
        (flat_index[None, :, :] == targets[:, None, None]).astype(jnp.int32),
        axis=2,
        dtype=jnp.int32,
    )
    return jnp.dot(select.astype(jnp.bfloat16), normed, preferred_element_type=jnp.float32).astype(
        jnp.bfloat16
    )


def combine(tokens, normed, gate_row, router_weight, block_ids, flat_index, expert_out):
    logits = jnp.dot(normed, router_weight, preferred_element_type=jnp.float32)
    picked = jnp.take_along_axis(logits, block_ids, axis=1)
    gap = picked[:, 0:1] - picked[:, 1:2]
    first = jnp.take(expert_out, flat_index[:, 0], axis=0).astype(jnp.float32)
    second = jnp.take(expert_out, flat_index[:, 1], axis=0).astype(jnp.float32)
    branch = jax.nn.sigmoid(gap) * first + jax.nn.sigmoid(-gap) * second
    return (tokens.astype(jnp.float32) + gate_row[None, :] * branch).astype(jnp.bfloat16)


def expert_compute(incoming, w_in, b_in, w_out):
    columns = incoming
    pre_act = jnp.einsum(
        "urd,udf->urf",
        columns,
        lax.all_gather(w_in, "fs", axis=1, tiled=True),
        preferred_element_type=jnp.float32,
    )
    hidden = jax.nn.gelu(pre_act + b_in[:, None, :], approximate=True).astype(jnp.bfloat16)
    columns = hidden
    produced = jnp.einsum(
        "urf,ufd->urd",
        columns,
        lax.all_gather(w_out, "fs", axis=1, tiled=True),
        preferred_element_type=jnp.float32,
    )
    return produced.astype(jnp.bfloat16)


def gathered_weights(
    hidden_states, expert_ids, modulation, router_weight, w_in, b_in, w_out
):
    token_count = hidden_states.shape[1]
    width = hidden_states.shape[2]
    tokens = hidden_states.reshape(token_count, width)
    block_ids = expert_ids.reshape(token_count, 2)
    settings = modulation[0]
    normed = modulate(tokens, settings[0][None, :], settings[1][None, :])
    flat_index = slot_index(block_ids)
    outgoing = dispatch_rows(normed, flat_index)
    per_expert = outgoing.reshape(EXPERTS, CAP, width)
    members = lax.axis_size("ep")
    local_units = w_in.shape[0]
    paired = local_units == 1
    half_cap = CAP // 2
    if paired:
        sending = per_expert.reshape(members, half_cap, width)
    else:
        sending = per_expert
    received = lax.all_to_all(sending, "ep", split_axis=0, concat_axis=1, tiled=True)
    if paired:
        parity = lax.axis_index("ep") % 2
        partner = swapped(received, "ep", 0)
        own_blocks = received.reshape(members, half_cap, width)
        other_blocks = partner.reshape(members, half_cap, width)
        lower = jnp.where(parity == 0, own_blocks, other_blocks)
        upper = jnp.where(parity == 0, other_blocks, own_blocks)
        incoming = jnp.stack([lower, upper], axis=1).reshape(1, members * CAP, width)
    else:
        incoming = jnp.repeat(received, SPLIT, axis=0)
    produced = expert_compute(incoming, w_in, b_in, w_out)
    if paired:
        halves = produced.reshape(members, 2, half_cap, width)
        kept_rows = jnp.where(parity == 0, halves[:, 0], halves[:, 1])
        given_rows = jnp.where(parity == 0, halves[:, 1], halves[:, 0])
        partner_out = swapped(given_rows, "ep", 0)
        reply = (kept_rows.astype(jnp.float32) + partner_out.astype(jnp.float32)).astype(
            jnp.bfloat16
        )
    else:
        local_experts = local_units // SPLIT
        summed = jnp.sum(
            produced.astype(jnp.float32).reshape(local_experts, SPLIT, members, CAP, width), axis=1
        )
        reply = (
            summed.astype(jnp.bfloat16)
            .transpose(1, 0, 2, 3)
            .reshape(members, local_experts * CAP, width)
        )
    returned = lax.all_to_all(reply, "ep", split_axis=0, concat_axis=0, tiled=True)
    expert_out = returned.reshape(EXPERTS, CAP, width)
    result = combine(
        tokens,
        normed,
        settings[2],
        router_weight,
        block_ids,
        flat_index,
        expert_out.reshape(EXPERTS * CAP, width),
    )
    return result.reshape(1, token_count, width)


def expert_kernel(
    place_ref, x_ref, own_ref, near_ref, far0_ref, far1_ref, cross_ref, b_ref, out_w_ref,
    keep_ref, send_ref, weight, total,
):
    step = pl.program_id(0)
    here, core = place_ref[0], place_ref[2]
    depth, columns = own_ref.shape[1], own_ref.shape[2]

    def rows(device):
        return pl.ds(pl.multiple_of(device * depth, depth), depth)

    weight[rows(here), :] = own_ref[0]
    weight[rows(here ^ 1), :] = near_ref[0]
    weight[rows(here ^ 3), :] = cross_ref[0]
    for number, far_ref in enumerate((far0_ref, far1_ref)):
        for half in range(2):

            @pl.when((step == number) & (core == half))
            def _(far_ref=far_ref, half=half):
                weight[rows(here ^ 2), :] = far_ref[0, :, half * columns : (half + 1) * columns]

    x = x_ref[...].reshape(-1, x_ref.shape[-1])
    pre = jnp.dot(x, weight[...], preferred_element_type=jnp.float32) + b_ref[0]
    hidden = jax.nn.gelu(pre, approximate=True).astype(jnp.bfloat16)
    piece = jnp.dot(hidden, out_w_ref[0], preferred_element_type=jnp.float32)
    half_rows = piece.shape[0] // 2

    @pl.when(step == 0)
    def _():
        total[...] = piece

    @pl.when(step == 1)
    def _():
        keep_ref[...] = total[:half_rows, :] + piece[:half_rows, :]
        send_ref[...] = (total[half_rows:, :] + piece[half_rows:, :]).astype(jnp.bfloat16)


def expert_call(expert, place, x, own, near, far0, far1, cross, b, w_out):
    images, _, rows, width = x.shape
    _, depth, columns = own.shape
    all_rows = images * rows

    def unit(step, place):
        return SPLIT * expert + (step ^ place[1])

    return pl.pallas_call(
        expert_kernel,
        grid_spec=pltpu.PrefetchScalarGridSpec(
            num_scalar_prefetch=1,
            grid=(SPLIT,),
            in_specs=[
                pl.BlockSpec((images, 1, rows, width), lambda s, p: (0, expert, 0, 0)),
                pl.BlockSpec((1, depth, columns), lambda s, p: (unit(s, p), 0, 0)),
                pl.BlockSpec((1, depth, columns), lambda s, p: (unit(s, p), 0, 0)),
                pl.BlockSpec((1, depth, 2 * columns), lambda s, p: (0, 0, 0)),
                pl.BlockSpec((1, depth, 2 * columns), lambda s, p: (0, 0, 0)),
                pl.BlockSpec((1, depth, columns), lambda s, p: (s, 0, 0)),
                pl.BlockSpec((1, 1, columns), lambda s, p: (unit(s, p), 0, 0)),
                pl.BlockSpec((1, columns, width), lambda s, p: (unit(s, p), 0, 0)),
            ],
            out_specs=[
                pl.BlockSpec((all_rows // 2, width), lambda s, p: (0, 0)),
                pl.BlockSpec((all_rows // 2, width), lambda s, p: (0, 0)),
            ],
            scratch_shapes=[
                pltpu.VMEM((width, columns), jnp.bfloat16),
                pltpu.VMEM((all_rows, width), jnp.float32),
            ],
        ),
        out_shape=[
            jax.ShapeDtypeStruct((all_rows // 2, width), jnp.float32),
            jax.ShapeDtypeStruct((all_rows // 2, width), jnp.bfloat16),
        ],
        compiler_params=pltpu.CompilerParams(vmem_limit_bytes=40 << 20),
        cost_estimate=pl.CostEstimate(
            flops=2 * SPLIT * 2 * all_rows * width * columns,
            bytes_accessed=2 * SPLIT * 2 * width * columns + 8 * all_rows * width,
            transcendentals=SPLIT * all_rows * columns,
        ),
        name="expert",
    )(place, x, own, near, far0, far1, cross, b, w_out)


def recut_weights(hidden_states, expert_ids, modulation, router_weight, w_in, b_in, w_out):
    token_count, width = hidden_states.shape[1:]
    units, depth, _ = w_in.shape
    columns = w_out.shape[1]
    experts = units // SPLIT
    members = lax.axis_size("ep")
    here, part = lax.axis_index("fs"), lax.axis_index("parts")
    core, chip = here & 1, here >> 1
    place = jnp.stack([here, part, core]).astype(jnp.int32)

    far = []
    for expert in range(experts):
        block = lax.dynamic_slice(
            w_in,
            (SPLIT * expert + part, 0, (1 - chip) * 2 * columns),
            (1, depth, 2 * columns),
        )
        far.append(swapped(block, "fs", 1))
    near = swapped(
        lax.dynamic_slice(w_in, (0, 0, (here ^ 1) * columns), (units, depth, columns)), "fs", 0
    )
    own = lax.dynamic_slice(w_in, (0, 0, here * columns), (units, depth, columns))
    other = [swapped(block, "parts", 0) for block in far]
    cross = [
        swapped(
            lax.dynamic_slice(
                jnp.concatenate([far[e], other[e]]),
                (0, 0, (1 - core) * columns),
                (SPLIT, depth, columns),
            ),
            "fs",
            0,
        )
        for e in range(experts)
    ]
    own_b = lax.dynamic_slice(b_in, (0, here * columns), (units, columns))[:, None, :]

    tokens = hidden_states.reshape(token_count, width)
    block_ids = expert_ids.reshape(token_count, 2)
    settings = modulation[0]
    normed = modulate(tokens, settings[0][None, :], settings[1][None, :])
    flat_index = slot_index(block_ids)
    listed = lax.all_gather(flat_index.T, ("fs", "ep"), axis=0, tiled=False)
    listed = listed.reshape(-1, members, 2, token_count)
    order = here ^ jnp.array([0, 2, 1, 3], jnp.int32)
    listed = jnp.take(listed, order, axis=0).transpose(0, 2, 1, 3).reshape(4, 2, 1, -1)
    opposite = swapped(normed, "fs", 1)
    mine = lax.all_gather(normed, "ep", axis=0, tiled=True)
    theirs = lax.all_gather(opposite, "ep", axis=0, tiled=True)
    same_core = jnp.stack([mine, theirs])
    other_core = swapped(same_core, "fs", 0)
    everyone = jnp.concatenate([same_core, other_core])
    target = jnp.arange(experts * members * CAP, dtype=jnp.int32)[:, None]
    owner = lax.axis_index("ep") * experts + target // (members * CAP)
    wanted = owner * CAP + target % CAP
    block_of = jnp.arange(members * token_count, dtype=jnp.int32)[None, :] // token_count
    in_block = (target // CAP) % members == block_of
    select = ((listed[:, 0] == wanted) | (listed[:, 1] == wanted)) & in_block
    x = jnp.einsum(
        "irt,itd->ird",
        select.astype(jnp.bfloat16),
        everyone,
        preferred_element_type=jnp.float32,
    ).astype(jnp.bfloat16)
    x = x.reshape(4, experts, members * CAP, width)

    returned = []
    for e in range(experts):
        keep, send = expert_call(
            e, place, x, own, near, far[e], other[e], cross[e], own_b, w_out
        )
        half = keep + swapped(send, "fs", 0).astype(jnp.float32)
        rows = members * CAP
        across = swapped(half[rows:].astype(jnp.bfloat16), "fs", 1)
        whole = (half[:rows] + across.astype(jnp.float32)).astype(jnp.bfloat16)
        returned.append(
            lax.all_to_all(
                whole.reshape(members, CAP, width), "ep", split_axis=0, concat_axis=0, tiled=True
            )
        )
    expert_out = jnp.stack(returned, axis=1).reshape(EXPERTS * CAP, width)
    result = combine(
        tokens, normed, settings[2], router_weight, block_ids, flat_index, expert_out
    )
    return result.reshape(1, token_count, width)


def local(*arrays):
    w_in = arrays[4]
    recut = (
        lax.axis_size("fs") == 4 and lax.axis_size("parts") == 2 and w_in.shape[0] % SPLIT == 0
    )
    return (recut_weights if recut else gathered_weights)(*arrays)


def solution(mesh):
    placed = (
        P(("parts", "fs"), "ep", None),
        P(("parts", "fs"), "ep", None),
        P(("parts", "fs"), None, None),
        P(),
        P("ep", "fs", None),
        P("ep", None),
        P("ep", "fs", None),
    )
    return jax.shard_map(
        local, mesh=mesh, in_specs=placed, out_specs=P(("parts", "fs"), "ep", None), check_vma=False
    )
```

```python
import functools

import jax
import jax.numpy as jnp
from jax import lax
from jax.experimental import pallas as pl
from jax.experimental.pallas import tpu as pltpu
from jax.sharding import PartitionSpec as P

EXPERTS = 16
SPLIT = 2
CAP = 20


norm_eps = 1e-06


def swapped(block, axis, distance):
    count = lax.axis_size(axis)
    route = []
    for low in range(count):
        high = low | 1 << distance
        if high != low and high < count:
            route += [(low, high), (high, low)]
    return lax.ppermute(block, axis, route)


def modulate(tokens, shift, scale):
    values = tokens.astype(jnp.float32)
    center = jnp.mean(values, axis=-1, keepdims=True)
    spread = jnp.mean(jnp.square(values - center), axis=-1, keepdims=True)
    normal = (values - center) * lax.rsqrt(spread + norm_eps)
    return (normal * (1.0 + scale) + shift).astype(jnp.bfloat16)


def slot_index(block_ids):
    flat_ids = block_ids.reshape(-1)
    one_hot = (flat_ids[:, None] == jnp.arange(EXPERTS, dtype=jnp.int32)[None, :]).astype(jnp.int32)
    earlier = jnp.cumsum(one_hot, axis=0, dtype=jnp.int32) - one_hot
    slots = jnp.sum(earlier * one_hot, axis=1, dtype=jnp.int32)
    return (flat_ids * CAP + slots).reshape(block_ids.shape)


def dispatch_rows(normed, flat_index):
    targets = jnp.arange(EXPERTS * CAP, dtype=jnp.int32)
    select = jnp.sum(
        (flat_index[None, :, :] == targets[:, None, None]).astype(jnp.int32),
        axis=2,
        dtype=jnp.int32,
    )
    return jnp.dot(select.astype(jnp.bfloat16), normed, preferred_element_type=jnp.float32).astype(
        jnp.bfloat16
    )


def combine(tokens, normed, gate_row, router_weight, block_ids, flat_index, expert_out):
    logits = jnp.dot(normed, router_weight, preferred_element_type=jnp.float32)
    picked = jnp.take_along_axis(logits, block_ids, axis=1)
    gap = picked[:, 0:1] - picked[:, 1:2]
    first = jnp.take(expert_out, flat_index[:, 0], axis=0).astype(jnp.float32)
    second = jnp.take(expert_out, flat_index[:, 1], axis=0).astype(jnp.float32)
    branch = jax.nn.sigmoid(gap) * first + jax.nn.sigmoid(-gap) * second
    return (tokens.astype(jnp.float32) + gate_row[None, :] * branch).astype(jnp.bfloat16)


def expert_compute(incoming, w_in, b_in, w_out):
    columns = incoming
    pre_act = jnp.einsum(
        "urd,udf->urf",
        columns,
        lax.all_gather(w_in, "fs", axis=1, tiled=True),
        preferred_element_type=jnp.float32,
    )
    hidden = jax.nn.gelu(pre_act + b_in[:, None, :], approximate=True).astype(jnp.bfloat16)
    columns = hidden
    produced = jnp.einsum(
        "urf,ufd->urd",
        columns,
        lax.all_gather(w_out, "fs", axis=1, tiled=True),
        preferred_element_type=jnp.float32,
    )
    return produced.astype(jnp.bfloat16)


def gathered_weights(
    hidden_states, expert_ids, modulation, router_weight, w_in, b_in, w_out
):
    token_count = hidden_states.shape[1]
    width = hidden_states.shape[2]
    tokens = hidden_states.reshape(token_count, width)
    block_ids = expert_ids.reshape(token_count, 2)
    settings = modulation[0]
    normed = modulate(tokens, settings[0][None, :], settings[1][None, :])
    flat_index = slot_index(block_ids)
    outgoing = dispatch_rows(normed, flat_index)
    per_expert = outgoing.reshape(EXPERTS, CAP, width)
    members = lax.axis_size("ep")
    local_units = w_in.shape[0]
    paired = local_units == 1
    half_cap = CAP // 2
    if paired:
        sending = per_expert.reshape(members, half_cap, width)
    else:
        sending = per_expert
    received = lax.all_to_all(sending, "ep", split_axis=0, concat_axis=1, tiled=True)
    if paired:
        parity = lax.axis_index("ep") % 2
        partner = swapped(received, "ep", 0)
        own_blocks = received.reshape(members, half_cap, width)
        other_blocks = partner.reshape(members, half_cap, width)
        lower = jnp.where(parity == 0, own_blocks, other_blocks)
        upper = jnp.where(parity == 0, other_blocks, own_blocks)
        incoming = jnp.stack([lower, upper], axis=1).reshape(1, members * CAP, width)
    else:
        incoming = jnp.repeat(received, SPLIT, axis=0)
    produced = expert_compute(incoming, w_in, b_in, w_out)
    if paired:
        halves = produced.reshape(members, 2, half_cap, width)
        kept_rows = jnp.where(parity == 0, halves[:, 0], halves[:, 1])
        given_rows = jnp.where(parity == 0, halves[:, 1], halves[:, 0])
        partner_out = swapped(given_rows, "ep", 0)
        reply = (kept_rows.astype(jnp.float32) + partner_out.astype(jnp.float32)).astype(
            jnp.bfloat16
        )
    else:
        local_experts = local_units // SPLIT
        summed = jnp.sum(
            produced.astype(jnp.float32).reshape(local_experts, SPLIT, members, CAP, width), axis=1
        )
        reply = (
            summed.astype(jnp.bfloat16)
            .transpose(1, 0, 2, 3)
            .reshape(members, local_experts * CAP, width)
        )
    returned = lax.all_to_all(reply, "ep", split_axis=0, concat_axis=0, tiled=True)
    expert_out = returned.reshape(EXPERTS, CAP, width)
    result = combine(
        tokens,
        normed,
        settings[2],
        router_weight,
        block_ids,
        flat_index,
        expert_out.reshape(EXPERTS * CAP, width),
    )
    return result.reshape(1, token_count, width)


def crossed(block, axis, mask):
    count = lax.axis_size(axis)
    return lax.ppermute(block, axis, [(i, i ^ mask) for i in range(count)])


def after(value, *events):
    return lax.optimization_barrier((value, *events))[0] if events else value


def slot_rows(ids, experts_count):
    tokens = ids[0].shape[1]
    experts = lax.broadcasted_iota(jnp.int32, (experts_count, tokens), 0).astype(jnp.float32)
    chosen = [jnp.where(experts == row, 1.0, 0.0) for row in ids]
    earlier = jnp.where(
        lax.broadcasted_iota(jnp.int32, (tokens, tokens), 0)
        < lax.broadcasted_iota(jnp.int32, (tokens, tokens), 1),
        1.0,
        0.0,
    )
    before = jnp.dot(
        (chosen[0] + chosen[1]).astype(jnp.bfloat16),
        earlier.astype(jnp.bfloat16),
        preferred_element_type=jnp.float32,
    )
    return [jnp.sum(before * one, axis=0, keepdims=True) for one in chosen]


def prepare_kernel(tokens_ref, ids_ref, settings_ref, out_ref):
    count, width = tokens_ref.shape[1:]
    out_ref[:count, :] = modulate(
        tokens_ref[0], settings_ref[0, 0:1, :], settings_ref[0, 1:2, :]
    )
    lanes = lax.broadcasted_iota(jnp.int32, (count, count), 1)
    columns = ids_ref[0].astype(jnp.float32)
    spread = jnp.where(lanes == 0, columns[:, 0:1], columns[:, 1:2]).T
    ids = [spread[0:1, :], spread[1:2, :]]
    listed = [*ids, *slot_rows(ids, EXPERTS), jnp.zeros((1, width - 4 * count), jnp.float32)]
    row = jnp.concatenate(listed, axis=1)
    first = lax.broadcasted_iota(jnp.int32, (16, width), 0) == 0
    out_ref[count:, :] = jnp.where(first, row, 0.0).astype(jnp.bfloat16)


def prepare_call(hidden_states, expert_ids, modulation):
    count, width = hidden_states.shape[1:]
    return pl.pallas_call(
        prepare_kernel,
        out_shape=jax.ShapeDtypeStruct((count + 16, width), jnp.bfloat16),
        name="prepare",
    )(hidden_states, expert_ids, modulation)


def route_kernel(block_ref, ids_ref, router_ref, out_ref):
    count = out_ref.shape[0]
    listed = block_ref[count:, :].astype(jnp.float32)[0:1, :]
    rows = [listed[:, k * count : (k + 1) * count] for k in range(4)]
    place = lax.broadcasted_iota(jnp.int32, (count, count), 0)
    spread = jnp.zeros((count, count), jnp.float32)
    for k, row in enumerate(rows):
        spread = jnp.where(place == k, row, spread)
    columns = spread.T
    logits = jnp.dot(block_ref[:count, :], router_ref[...], preferred_element_type=jnp.float32)
    ids = ids_ref[0]
    experts = lax.broadcasted_iota(jnp.int32, logits.shape, 1)
    picked = [
        jnp.sum(jnp.where(experts == ids[:, k : k + 1], logits, 0.0), axis=1, keepdims=True)
        for k in range(2)
    ]
    gap = picked[0] - picked[1]
    lanes = lax.broadcasted_iota(jnp.int32, (count, count), 1)
    columns = jnp.where(lanes == 4, jax.nn.sigmoid(gap), columns)
    out_ref[...] = jnp.where(lanes == 5, jax.nn.sigmoid(-gap), columns)


def route_call(block, expert_ids, router_weight):
    count = expert_ids.shape[1]
    return pl.pallas_call(
        route_kernel,
        out_shape=jax.ShapeDtypeStruct((count, count), jnp.float32),
        name="route",
    )(block, expert_ids, router_weight)


def dispatch_kernel(wanted_ref, *refs):
    images = wanted_ref.shape[1]
    blocks, outs = refs[:images], refs[images:]
    rows = outs[0].shape[0]
    count = blocks[0].shape[0] - 16
    choices = []
    for image, block in enumerate(blocks):
        listed = block[count:, :].astype(jnp.float32)[0:1, :]
        wanted = wanted_ref[:, image : image + 1]
        chosen = None
        for k in range(2):
            ids = listed[:, k * count : (k + 1) * count]
            slots = listed[:, (2 + k) * count : (3 + k) * count]
            match = wanted == ids * CAP + slots
            chosen = match if chosen is None else chosen | match
        choices.append(jnp.where(chosen, 1.0, 0.0).astype(jnp.bfloat16))
    select = jnp.concatenate(choices, axis=1)
    tokens = jnp.concatenate([block[:count, :] for block in blocks], axis=0)
    for number, out_ref in enumerate(outs):
        out_ref[...] = jnp.dot(
            select[number * rows : (number + 1) * rows, :],
            tokens,
            preferred_element_type=jnp.float32,
        ).astype(jnp.bfloat16)


def dispatch_call(wanted, blocks, members):
    rows = wanted.shape[0] // members
    width = blocks[0].shape[1]
    return pl.pallas_call(
        dispatch_kernel,
        out_shape=[jax.ShapeDtypeStruct((rows, width), jnp.bfloat16)] * members,
        name="dispatch",
    )(wanted, *blocks)


def cut_kernel(plan, place_ref, w_in_ref, *refs):
    outs, (held, sems) = refs[:-2], refs[-2:]
    width = held.shape[2]
    chip = place_ref[0] >> 1
    arriving, leaving = [], []
    for number, (unit, offset, rows, far) in enumerate(plan):
        first = pl.multiple_of((1 - chip if far else chip) * width, 128)
        count = outs[number].shape[0]
        for at in range(count):
            slot = len(arriving)
            source = w_in_ref.at[
                unit + (place_ref[1] if far else at), pl.ds(offset, rows), pl.ds(first, width)
            ]
            staged = held.at[slot, pl.ds(0, rows), :]
            arriving.append(pltpu.make_async_copy(source, staged, sems.at[0, slot]))
            leaving.append(pltpu.make_async_copy(staged, outs[number].at[at], sems.at[1, slot]))
    for copy in arriving:
        copy.start()
    for copy, onward in zip(arriving, leaving, strict=True):
        copy.wait()
        onward.start()
    for copy in leaving:
        copy.wait()


def cut_call(plan, width, place, w_in):
    anywhere = pl.BlockSpec(memory_space=pl.ANY)
    slots = sum(1 if far else SPLIT for *_, far in plan)
    return pl.pallas_call(
        functools.partial(cut_kernel, plan),
        in_specs=[pl.BlockSpec(memory_space=pltpu.SMEM), anywhere],
        out_specs=[anywhere] * len(plan),
        out_shape=[
            jax.ShapeDtypeStruct((1 if far else SPLIT, rows, width), jnp.bfloat16)
            for _, _, rows, far in plan
        ],
        scratch_shapes=[
            pltpu.VMEM((slots, w_in.shape[1], width), jnp.bfloat16),
            pltpu.SemaphoreType.DMA((2, slots)),
        ],
        compiler_params=pltpu.CompilerParams(vmem_limit_bytes=60 << 20),
        name="cut",
    )(place, w_in)


def expert_kernel(
    expert, groups, sources, place_ref, own_ref, b_ref, out_w_ref, *refs
):
    x_refs, refs = refs[:sources], refs[sources:]
    arrays, refs = refs[:-10], refs[-10:]
    near_ref, keep_ref, keep_far_ref, send_ref, *refs = refs
    x_pairs, x_held, weight, out_weight, total, sems = refs
    step = pl.program_id(0)
    here, part, core = place_ref[0], place_ref[1], place_ref[2]
    depth = own_ref.shape[1]
    columns, width = out_w_ref.shape[1:]
    slab = weight.shape[2]
    skip = slab - columns
    wide = 2 * columns
    first = pl.multiple_of(core * (wide - slab), 128)
    chip_first = pl.multiple_of((here >> 1) * wide + core * (wide - slab), 128)
    half_rows = x_held.shape[0] // 2
    per = x_pairs.shape[1] // 2

    def copies(number):
        unit = SPLIT * expert + (number ^ part)
        made = []

        def add(source, target):
            made.append(pltpu.make_async_copy(source, target, sems.at[number, len(made)]))

        def rows(device, offset, size):
            return weight.at[number, pl.ds(pl.multiple_of(device * depth + offset, 16), size), :]

        add(own_ref.at[unit, :, pl.ds(chip_first, slab)], rows(here, 0, depth))
        add(near_ref.at[number ^ part, :, pl.ds(first, slab)], rows(here ^ 1, 0, depth))
        for relative, at, offset, size in groups[number]:
            add(
                arrays[at].at[0, :, pl.ds(first, slab)],
                rows(here ^ relative, offset, size),
            )
        add(
            out_w_ref.at[unit],
            out_weight.at[number, pl.ds(pl.multiple_of(core * skip, 16), columns), :],
        )
        return made

    spare_sem = sems.shape[1] - sources
    x_copies = [
        pltpu.make_async_copy(
            x_ref.at[pl.ds(2 * per * (expert // 2), 2 * per), :],
            x_pairs.at[at],
            sems.at[0, spare_sem + at],
        )
        for at, x_ref in enumerate(x_refs)
    ]

    @pl.when(step == 0)
    def _():
        for copy in x_copies:
            copy.start()
        for number in range(SPLIT):
            for copy in copies(number):
                copy.start()
        for number in range(SPLIT):
            spare = pl.ds(pl.multiple_of((1 - core) * columns, 16), skip)
            out_weight[number, spare, :] = jnp.zeros((skip, width), out_weight.dtype)
        for at, copy in enumerate(x_copies):
            copy.wait()
            pair = x_pairs[at].astype(jnp.float32)
            own_rows = pair[per * (expert % 2) : per * (expert % 2 + 1), :]
            total[per * at : per * (at + 1), :] = own_rows
        x_held[...] = total[...].astype(jnp.bfloat16)

    for number in range(SPLIT):

        @pl.when(step == number)
        def _(number=number):
            for copy in copies(number):
                copy.wait()

    pre = jnp.dot(x_held[...], weight[step], preferred_element_type=jnp.float32) + b_ref[0]
    hidden = jax.nn.gelu(pre, approximate=True).astype(jnp.bfloat16)
    piece = jnp.dot(hidden, out_weight[step], preferred_element_type=jnp.float32)

    @pl.when(step == 0)
    def _():
        total[...] = piece

    @pl.when(step == 1)
    def _():
        total[...] += piece
        members = half_rows // (2 * CAP)
        for member in range(members):
            at = 2 * CAP * member
            keep_ref[CAP * member : CAP * (member + 1), :] = total[at : at + CAP, :]
            keep_far_ref[CAP * member : CAP * (member + 1), :] = total[at + CAP : at + 2 * CAP, :]
        given = [
            total[at : at + CAP, :]
            for image in range(2)
            for at in range(half_rows + CAP * image, 2 * half_rows, 2 * CAP)
        ]
        for number, rows in enumerate(given):
            total[CAP * number : CAP * (number + 1), :] = rows
        send_ref[...] = total[:half_rows, :].astype(jnp.bfloat16)


def expert_call(expert, place, xs, own, b, w_out, near, pieces):
    width = w_out.shape[2]
    per = 2 * CAP
    half_rows = per * len(xs) // 2
    columns = w_out.shape[1]
    slab = b.shape[2]
    arrays, groups = [], [[] for _ in range(SPLIT)]
    for number, relative, array, offset in pieces:
        groups[number].append((relative, len(arrays), offset, array.shape[1]))
        arrays.append(array)
    anywhere = pl.BlockSpec(memory_space=pl.ANY)
    kept = pl.BlockSpec((half_rows // 2, width), lambda s, p: (0, 0))

    return pl.pallas_call(
        functools.partial(expert_kernel, expert, groups, len(xs)),
        grid_spec=pltpu.PrefetchScalarGridSpec(
            num_scalar_prefetch=1,
            grid=(SPLIT,),
            in_specs=[
                anywhere,
                pl.BlockSpec((1, 1, slab), lambda s, p: (SPLIT * expert + (s ^ p[1]), 0, 0)),
                anywhere,
                *([anywhere] * (len(xs) + len(arrays) + 1)),
            ],
            out_specs=[kept, kept, pl.BlockSpec((half_rows, width), lambda s, p: (0, 0))],
            scratch_shapes=[
                pltpu.VMEM((len(xs), 2 * per, width), jnp.bfloat16),
                pltpu.VMEM((2 * half_rows, width), jnp.bfloat16),
                pltpu.VMEM((SPLIT, width, slab), jnp.bfloat16),
                pltpu.VMEM((SPLIT, slab, width), jnp.bfloat16),
                pltpu.VMEM((2 * half_rows, width), jnp.float32),
                pltpu.SemaphoreType.DMA((SPLIT, 3 + max(map(len, groups)) + len(xs))),
            ],
        ),
        out_shape=[
            jax.ShapeDtypeStruct((half_rows // 2, width), jnp.float32),
            jax.ShapeDtypeStruct((half_rows // 2, width), jnp.float32),
            jax.ShapeDtypeStruct((half_rows, width), jnp.bfloat16),
        ],
        compiler_params=pltpu.CompilerParams(vmem_limit_bytes=60 << 20),
        cost_estimate=pl.CostEstimate(
            flops=2 * SPLIT * 2 * 2 * half_rows * width * columns,
            bytes_accessed=2 * SPLIT * 3 * width * columns + 16 * half_rows * width,
            transcendentals=SPLIT * 2 * half_rows * columns,
        ),
        name="expert",
    )(place, own, b, w_out, *xs, *arrays, near)


def combine_kernel(experts, groups, place_ref, route_ref, tokens_ref, settings_ref, *refs):
    out_ref, held = refs[-2:]
    replies = refs[:-2]
    count = route_ref.shape[0]
    members = len(replies) // len(groups)
    at = 0
    for reply in replies:
        rows = reply.shape[0]
        held[at : at + rows, :] = reply[...].astype(jnp.float32)
        at += rows
    rows_held = held[...].astype(jnp.bfloat16)
    place = lax.broadcasted_iota(jnp.int32, (count, at), 1)
    branch = None
    for k in range(2):
        expert = route_ref[:, k : k + 1].astype(jnp.int32)
        slot = route_ref[:, 2 + k : 3 + k].astype(jnp.int32)
        owner = jnp.zeros_like(expert)
        for member in range(1, members):
            owner += jnp.where(expert >= member * experts, 1, 0)
        local_expert = expert - owner * experts
        ring = owner ^ place_ref[3]
        position = jnp.zeros_like(expert)
        first = 0
        for group in groups:
            size = len(group) * CAP
            inside = (local_expert >= group[0]) & (local_expert <= group[-1])
            here = first + ring * size + (local_expert - group[0]) * CAP + slot
            position = jnp.where(inside, here, position)
            first += members * size
        select = jnp.where(place == position, 1.0, 0.0).astype(jnp.bfloat16)
        term = route_ref[:, 4 + k : 5 + k] * jnp.dot(
            select, rows_held, preferred_element_type=jnp.float32
        )
        branch = term if branch is None else branch + term
    out_ref[0] = (
        tokens_ref[0].astype(jnp.float32) + settings_ref[0, 2:3, :] * branch
    ).astype(out_ref.dtype)


def combine_call(experts, groups, place, route, hidden_states, modulation, replies):
    rows = sum(reply.shape[0] for reply in replies)
    whole = pl.BlockSpec(memory_space=pltpu.VMEM)
    return pl.pallas_call(
        functools.partial(combine_kernel, experts, groups),
        in_specs=[pl.BlockSpec(memory_space=pltpu.SMEM), *([whole] * (3 + len(replies)))],
        out_shape=jax.ShapeDtypeStruct(hidden_states.shape, hidden_states.dtype),
        scratch_shapes=[pltpu.VMEM((rows, hidden_states.shape[2]), jnp.float32)],
        name="combine",
    )(place, route, hidden_states, modulation, *replies)


def recut_weights(hidden_states, expert_ids, modulation, router_weight, w_in, b_in, w_out):
    units, depth, _ = w_in.shape
    columns = w_out.shape[1]
    wide = 2 * columns
    experts = units // SPLIT
    members = lax.axis_size("ep")
    here, part, row = lax.axis_index("fs"), lax.axis_index("parts"), lax.axis_index("ep")
    core, chip = here & 1, here >> 1
    place = jnp.stack([here, part, core, row]).astype(jnp.int32)

    plan = []
    for expert in range(experts):
        pieces = 2 if expert == experts - 1 else 1
        plan += [(expert, piece * (depth // pieces), depth // pieces) for piece in range(pieces)]

    def over(held, gate):
        return crossed(after(held, gate), "fs", 1)

    def beside(held, gate):
        return crossed(after(held, gate), "parts", 1)

    slab = -(-columns // 128) * 128
    own_b = lax.dynamic_slice(
        b_in, (0, chip * wide + core * (wide - slab)), (units, slab)
    )[:, None, :]
    per = 2 * CAP
    shape = (members, experts, 2, CAP)
    number = [jnp.broadcast_to(jnp.arange(size, dtype=jnp.int32).reshape(
        [-1 if axis == at else 1 for axis in range(4)]), shape).reshape(-1)
        for at, size in enumerate(shape)]
    wanted = ((row ^ number[0]) * experts + number[1]) * CAP + number[3]
    wanted = jnp.stack([jnp.where(number[2] == image, wanted, -1) for image in range(2)], axis=1)

    block = prepare_call(hidden_states, expert_ids, modulation)
    gate = after(place, block)
    cuts = cut_call(
        tuple((SPLIT * e, offset, rows, True) for e, offset, rows in plan)
        + tuple((SPLIT * e, 0, depth, False) for e in range(experts)),
        wide,
        place,
        w_in,
    )
    leaving, nearby = cuts[: len(plan)], cuts[len(plan) :]

    def fetch(number, gate):
        return crossed(after(leaving[number], gate), "fs", 2)

    opposite = crossed(after(block, gate), "fs", 2)
    gate = after(gate, opposite, leaving[0])
    far = [fetch(0, gate), fetch(1, gate)]
    sending = dispatch_call(wanted.astype(jnp.float32), [block, opposite], members)
    arrived = [sending[0]] + [crossed(sending[d], "ep", d) for d in range(1, members - 1)]
    across = [over(sending[0], gate)]
    gate = after(gate, far[0], across[0], *arrived[1:])

    far.append(fetch(2, gate))
    arrived.append(crossed(after(sending[-1], gate), "ep", members - 1))
    other = [beside(far[0], gate)]
    cross = [over(far[0], gate)]
    across += [over(held, gate) for held in arrived[1:-1]]
    near = [over(nearby[0], gate)]
    gate = after(gate, far[1], arrived[-1], other[0], cross[0], *across[1:])

    far.append(fetch(3, gate))
    other.append(beside(far[1], gate))
    cross.append(over(far[1], gate))
    cross_other = [over(other[0], gate)]
    across.append(over(arrived[-1], gate))
    near.append(over(nearby[1], gate))
    gate = after(gate, far[2], other[1], cross[1], cross_other[0], across[-1])

    far.append(fetch(4, gate))
    other.append(beside(far[2], gate))
    cross.append(over(far[2], gate))
    cross_other.append(over(other[1], gate))
    near.append(over(nearby[2], gate))

    def run(expert):
        pieces = []
        for at, (of, offset, _) in enumerate(plan):
            if of == expert:
                pieces += [(0, 2, far[at], offset), (0, 3, cross[at], offset)]
                pieces += [(1, 2, other[at], offset), (1, 3, cross_other[at], offset)]
        return expert_call(
            expert, place, arrived + across, w_in, own_b, w_out, near[expert], pieces
        )

    outs = [run(0)]
    gate = after(gate, far[3], cross[2], cross_other[1], outs[0][0])
    other.append(beside(far[3], gate))
    cross.append(over(far[3], gate))
    near.append(over(nearby[3], gate))
    cross_other.append(over(other[2], gate))
    outs.append(run(1))
    gate = after(gate, far[4], cross[3], cross_other[2], outs[1][0])
    other.append(beside(far[4], gate))
    cross.append(over(far[4], gate))
    cross_other.append(over(other[3], gate))
    outs.append(run(2))
    gate = after(gate, outs[2][0])
    cross_other.append(over(other[4], gate))
    outs.append(run(3))

    route = route_call(block, expert_ids, router_weight)
    half_rows = members * CAP
    sent = [crossed(send, "fs", 1) for _, _, send in outs]
    wholes = []
    for e in range(experts):
        keep, keep_far, _ = outs[e]
        given = (keep_far + sent[e][half_rows:].astype(jnp.float32)).astype(jnp.bfloat16)
        given = crossed(after(given, *[out[0] for out in outs[e + 1 : e + 2]]), "fs", 2)
        half = keep + sent[e][:half_rows].astype(jnp.float32)
        wholes.append((half + given.astype(jnp.float32)).astype(jnp.bfloat16))
    groups = ((0, 1), (2, 3))
    replies = []
    for group in groups:
        for d in range(members):
            reply = jnp.concatenate([wholes[e][d * CAP : (d + 1) * CAP] for e in group])
            reply = crossed(after(reply, outs[-1][0]), "ep", d) if d else reply
            replies.append(reply)
    return combine_call(experts, groups, place, route, hidden_states, modulation, replies)


def local(*arrays):
    w_in = arrays[4]
    recut = lax.axis_size("fs") == lax.axis_size("ep") == 4 and lax.axis_size("parts") == 2
    recut = recut and w_in.shape[0] == 4 * SPLIT
    return (recut_weights if recut else gathered_weights)(*arrays)


def solution(mesh):
    placed = (
        P(("parts", "fs"), "ep", None),
        P(("parts", "fs"), "ep", None),
        P(("parts", "fs"), None, None),
        P(),
        P("ep", "fs", None),
        P("ep", None),
        P("ep", "fs", None),
    )
    return jax.shard_map(
        local, mesh=mesh, in_specs=placed, out_specs=P(("parts", "fs"), "ep", None), check_vma=False
    )
```

```python
import functools

import jax
import jax.numpy as jnp
import numpy as np
from jax import lax
from jax.experimental import pallas as pl
from jax.experimental.pallas import tpu as pltpu
from jax.sharding import PartitionSpec as P

EXPERTS = 16
SPLIT = 2
CAP = 20


norm_eps = 1e-06


def swapped(block, axis, distance):
    count = lax.axis_size(axis)
    route = []
    for low in range(count):
        high = low | 1 << distance
        if high != low and high < count:
            route += [(low, high), (high, low)]
    return lax.ppermute(block, axis, route)


def modulate(tokens, shift, scale):
    values = tokens.astype(jnp.float32)
    center = jnp.mean(values, axis=-1, keepdims=True)
    spread = jnp.mean(jnp.square(values - center), axis=-1, keepdims=True)
    normal = (values - center) * lax.rsqrt(spread + norm_eps)
    return (normal * (1.0 + scale) + shift).astype(jnp.bfloat16)


def slot_index(block_ids):
    flat_ids = block_ids.reshape(-1)
    one_hot = (flat_ids[:, None] == jnp.arange(EXPERTS, dtype=jnp.int32)[None, :]).astype(jnp.int32)
    earlier = jnp.cumsum(one_hot, axis=0, dtype=jnp.int32) - one_hot
    slots = jnp.sum(earlier * one_hot, axis=1, dtype=jnp.int32)
    return (flat_ids * CAP + slots).reshape(block_ids.shape)


def dispatch_rows(normed, flat_index):
    targets = jnp.arange(EXPERTS * CAP, dtype=jnp.int32)
    select = jnp.sum(
        (flat_index[None, :, :] == targets[:, None, None]).astype(jnp.int32),
        axis=2,
        dtype=jnp.int32,
    )
    return jnp.dot(select.astype(jnp.bfloat16), normed, preferred_element_type=jnp.float32).astype(
        jnp.bfloat16
    )


def combine(tokens, normed, gate_row, router_weight, block_ids, flat_index, expert_out):
    logits = jnp.dot(normed, router_weight, preferred_element_type=jnp.float32)
    picked = jnp.take_along_axis(logits, block_ids, axis=1)
    gap = picked[:, 0:1] - picked[:, 1:2]
    first = jnp.take(expert_out, flat_index[:, 0], axis=0).astype(jnp.float32)
    second = jnp.take(expert_out, flat_index[:, 1], axis=0).astype(jnp.float32)
    branch = jax.nn.sigmoid(gap) * first + jax.nn.sigmoid(-gap) * second
    return (tokens.astype(jnp.float32) + gate_row[None, :] * branch).astype(jnp.bfloat16)


def expert_compute(incoming, w_in, b_in, w_out):
    columns = incoming
    pre_act = jnp.einsum(
        "urd,udf->urf",
        columns,
        lax.all_gather(w_in, "fs", axis=1, tiled=True),
        preferred_element_type=jnp.float32,
    )
    hidden = jax.nn.gelu(pre_act + b_in[:, None, :], approximate=True).astype(jnp.bfloat16)
    columns = hidden
    produced = jnp.einsum(
        "urf,ufd->urd",
        columns,
        lax.all_gather(w_out, "fs", axis=1, tiled=True),
        preferred_element_type=jnp.float32,
    )
    return produced.astype(jnp.bfloat16)


def gathered_weights(
    hidden_states, expert_ids, modulation, router_weight, w_in, b_in, w_out
):
    token_count = hidden_states.shape[1]
    width = hidden_states.shape[2]
    tokens = hidden_states.reshape(token_count, width)
    block_ids = expert_ids.reshape(token_count, 2)
    settings = modulation[0]
    normed = modulate(tokens, settings[0][None, :], settings[1][None, :])
    flat_index = slot_index(block_ids)
    outgoing = dispatch_rows(normed, flat_index)
    per_expert = outgoing.reshape(EXPERTS, CAP, width)
    members = lax.axis_size("ep")
    local_units = w_in.shape[0]
    paired = local_units == 1
    half_cap = CAP // 2
    if paired:
        sending = per_expert.reshape(members, half_cap, width)
    else:
        sending = per_expert
    received = lax.all_to_all(sending, "ep", split_axis=0, concat_axis=1, tiled=True)
    if paired:
        parity = lax.axis_index("ep") % 2
        partner = swapped(received, "ep", 0)
        own_blocks = received.reshape(members, half_cap, width)
        other_blocks = partner.reshape(members, half_cap, width)
        lower = jnp.where(parity == 0, own_blocks, other_blocks)
        upper = jnp.where(parity == 0, other_blocks, own_blocks)
        incoming = jnp.stack([lower, upper], axis=1).reshape(1, members * CAP, width)
    else:
        incoming = jnp.repeat(received, SPLIT, axis=0)
    produced = expert_compute(incoming, w_in, b_in, w_out)
    if paired:
        halves = produced.reshape(members, 2, half_cap, width)
        kept_rows = jnp.where(parity == 0, halves[:, 0], halves[:, 1])
        given_rows = jnp.where(parity == 0, halves[:, 1], halves[:, 0])
        partner_out = swapped(given_rows, "ep", 0)
        reply = (kept_rows.astype(jnp.float32) + partner_out.astype(jnp.float32)).astype(
            jnp.bfloat16
        )
    else:
        local_experts = local_units // SPLIT
        summed = jnp.sum(
            produced.astype(jnp.float32).reshape(local_experts, SPLIT, members, CAP, width), axis=1
        )
        reply = (
            summed.astype(jnp.bfloat16)
            .transpose(1, 0, 2, 3)
            .reshape(members, local_experts * CAP, width)
        )
    returned = lax.all_to_all(reply, "ep", split_axis=0, concat_axis=0, tiled=True)
    expert_out = returned.reshape(EXPERTS, CAP, width)
    result = combine(
        tokens,
        normed,
        settings[2],
        router_weight,
        block_ids,
        flat_index,
        expert_out.reshape(EXPERTS * CAP, width),
    )
    return result.reshape(1, token_count, width)


def crossed(block, axis, mask):
    count = lax.axis_size(axis)
    return lax.ppermute(block, axis, [(i, i ^ mask) for i in range(count)])


def after(value, *events):
    return lax.optimization_barrier((value, *events))[0] if events else value


def slot_rows(ids, experts_count):
    tokens = ids[0].shape[1]
    experts = lax.broadcasted_iota(jnp.int32, (experts_count, tokens), 0).astype(jnp.float32)
    chosen = [jnp.where(experts == row, 1.0, 0.0) for row in ids]
    earlier = jnp.where(
        lax.broadcasted_iota(jnp.int32, (tokens, tokens), 0)
        < lax.broadcasted_iota(jnp.int32, (tokens, tokens), 1),
        1.0,
        0.0,
    )
    before = jnp.dot(
        (chosen[0] + chosen[1]).astype(jnp.bfloat16),
        earlier.astype(jnp.bfloat16),
        preferred_element_type=jnp.float32,
    )
    return [jnp.sum(before * one, axis=0, keepdims=True) for one in chosen]


def prepare_kernel(tokens_ref, ids_ref, settings_ref, out_ref):
    count, width = tokens_ref.shape[1:]
    out_ref[:count, :] = modulate(tokens_ref[0], settings_ref[0:1, :], settings_ref[1:2, :])
    ids = [ids_ref[0:1, :], ids_ref[1:2, :]]
    listed = [*ids, *slot_rows(ids, EXPERTS), jnp.zeros((1, width - 4 * count), jnp.float32)]
    row = jnp.concatenate(listed, axis=1)
    first = lax.broadcasted_iota(jnp.int32, (16, width), 0) == 0
    out_ref[count:, :] = jnp.where(first, row, 0.0).astype(jnp.bfloat16)


def prepare_call(hidden_states, ids, settings):
    count, width = hidden_states.shape[1:]
    return pl.pallas_call(
        prepare_kernel,
        out_shape=jax.ShapeDtypeStruct((count + 16, width), jnp.bfloat16),
        name="prepare",
    )(hidden_states, ids, settings)


def route_kernel(block_ref, router_ref, out_ref):
    count = out_ref.shape[0]
    listed = block_ref[count:, :].astype(jnp.float32)[0:1, :]
    place = lax.broadcasted_iota(jnp.int32, (count, count), 0)
    spread = jnp.zeros((count, count), jnp.float32)
    for k in range(4):
        spread = jnp.where(place == k, listed[:, k * count : (k + 1) * count], spread)
    columns = spread.T
    logits = jnp.dot(block_ref[:count, :], router_ref[...], preferred_element_type=jnp.float32)
    experts = lax.broadcasted_iota(jnp.int32, logits.shape, 1).astype(jnp.float32)
    picked = [
        jnp.sum(jnp.where(experts == columns[:, k : k + 1], logits, 0.0), axis=1, keepdims=True)
        for k in range(2)
    ]
    gap = picked[0] - picked[1]
    lanes = lax.broadcasted_iota(jnp.int32, (count, count), 1)
    columns = jnp.where(lanes == 4, jax.nn.sigmoid(gap), columns)
    out_ref[...] = jnp.where(lanes == 5, jax.nn.sigmoid(-gap), columns)


def route_call(block, router_weight):
    count = block.shape[0] - 16
    return pl.pallas_call(
        route_kernel,
        out_shape=jax.ShapeDtypeStruct((count, count), jnp.float32),
        name="route",
    )(block, router_weight)


def dispatch_kernel(wanted_ref, *refs):
    rows, images = wanted_ref.shape
    blocks, outs = refs[:images], refs[images:]
    count = blocks[0].shape[0] - 16
    places = []
    for block in blocks:
        listed = block[count:, :].astype(jnp.float32)[0:1, :]
        parts = [listed[:, k * count : (k + 1) * count] for k in range(4)]
        places.append([parts[k] * CAP + parts[2 + k] for k in range(2)])
    tokens = jnp.concatenate([block[:count, :] for block in blocks], axis=0)
    owner = lax.axis_index("ep")
    for number, out_ref in enumerate(outs):
        first = (owner ^ number) * (rows // images)
        choices = []
        for image in range(images):
            wanted = wanted_ref[:, image : image + 1] + first.astype(jnp.float32)
            match = (wanted == places[image][0]) | (wanted == places[image][1])
            choices.append(jnp.where(match, 1.0, 0.0).astype(jnp.bfloat16))
        out_ref[...] = jnp.dot(
            jnp.concatenate(choices, axis=1), tokens, preferred_element_type=jnp.float32
        ).astype(jnp.bfloat16)


def dispatch_call(wanted, blocks, members):
    rows = wanted.shape[0]
    width = blocks[0].shape[1]
    return pl.pallas_call(
        dispatch_kernel,
        out_shape=[jax.ShapeDtypeStruct((rows, width), jnp.bfloat16)] * members,
        cost_estimate=pl.CostEstimate(
            flops=2 * members * rows * len(blocks) * blocks[0].shape[0] * width,
            bytes_accessed=4 * members * rows * width,
            transcendentals=0,
        ),
        name="dispatch",
    )(wanted, *blocks)


def halves_turned(tile):
    half = tile.shape[1] // 2
    return pltpu.roll(tile.astype(jnp.float32), half, 1).astype(tile.dtype)


def where_am_i():
    here, part = lax.axis_index("fs"), lax.axis_index("parts")
    return here, part, here & 1


def cut_kernel(groups, w_in_ref, *refs):
    outs, (held, tiles, sems) = refs[:-3], refs[-3:]
    experts, depth, lanes = tiles.shape
    upper = depth // 2
    slots = [(g, at) for g, group in enumerate(groups) for at in range(len(group))]
    wide = held.shape[2]
    main = (wide - lanes) // 2
    here, part, core = where_am_i()
    chip = here >> 1
    first = (1 - chip) * wide
    rest = [
        pltpu.make_async_copy(
            w_in_ref.at[SPLIT * e + part, :, pl.ds(pl.multiple_of(first + main, 128), lanes)],
            tiles.at[e],
            sems.at[0, e],
        )
        for e in range(experts)
    ]
    arriving, leaving = [], []
    for number in range(2 * experts):
        e, target = number // 2, core ^ (number % 2)
        group, at = slots[e]
        out = outs[2 * group + number % 2].at[pl.ds(at * upper, upper), :]
        columns = pl.ds(pl.multiple_of(first + target * (main + lanes), 128), main)
        arriving.append(
            [
                pltpu.make_async_copy(
                    w_in_ref.at[SPLIT * e + part, pl.ds(half * upper, upper), columns],
                    held.at[number, :, pl.ds(half * main, main)],
                    sems.at[1 + half, number],
                )
                for half in range(2)
            ]
        )
        leaving.append(pltpu.make_async_copy(held.at[number], out, sems.at[3, number]))
    for copy in rest:
        copy.start()
    for halves in arriving:
        for copy in halves:
            copy.start()
    left = lax.broadcasted_iota(jnp.int32, (upper, lanes), 1) < lanes // 2
    for number, halves in enumerate(arriving):
        e, target = number // 2, core ^ (number % 2)
        if number % 2 == 0:
            rest[e].wait()
        top, bottom = tiles[e, :upper, :], tiles[e, upper:, :]
        low = jnp.where(left, top, halves_turned(bottom))
        high = jnp.where(left, halves_turned(top), bottom)
        held[number, :, 2 * main :] = jnp.where(target == 0, low, high)
        for copy in halves:
            copy.wait()
        leaving[number].start()
    for copy in leaving:
        copy.wait()


def cut_call(w_in, wide, groups):
    units, depth, _ = w_in.shape
    experts = units // SPLIT
    anywhere = pl.BlockSpec(memory_space=pl.ANY)
    blocks = 2 * experts
    return pl.pallas_call(
        functools.partial(cut_kernel, groups),
        in_specs=[anywhere],
        out_specs=[anywhere] * (2 * len(groups)),
        out_shape=[
            jax.ShapeDtypeStruct((len(group) * (depth // 2), wide), jnp.bfloat16)
            for group in groups
            for _ in range(2)
        ],
        scratch_shapes=[
            pltpu.VMEM((blocks, depth // 2, wide), jnp.bfloat16),
            pltpu.VMEM((experts, depth, 128), jnp.bfloat16),
            pltpu.SemaphoreType.DMA((4, blocks)),
        ],
        compiler_params=pltpu.CompilerParams(vmem_limit_bytes=60 << 20),
        cost_estimate=pl.CostEstimate(
            flops=0, bytes_accessed=4 * blocks * (depth // 2) * wide, transcendentals=0
        ),
        name="cut",
    )(w_in)


def expert_kernel(expert, sources, offsets, events, own_ref, b_ref, out_w_ref, *refs):
    x_refs, refs = refs[:sources], refs[sources:]
    near_ref, moved_refs, refs = refs[0], refs[1:5], refs[5 + events :]
    keep_ref, keep_far_ref, send_ref, *refs = refs
    x_pairs, x_held, weight, rest, bias, out_weight, total, sems = refs
    here, part, core = where_am_i()
    depth = own_ref.shape[1]
    columns, width = out_w_ref.shape[1:]
    upper, lanes = rest.shape[2:]
    slab = weight.shape[2]
    skip = slab - columns
    wide = 2 * columns
    main = slab - lanes
    chip_first = pl.multiple_of((here >> 1) * wide + core * (wide - slab), 128)
    half_rows = x_held.shape[0] // 2
    per = x_pairs.shape[1] // 2

    def rows(device, offset, size):
        return pl.ds(pl.multiple_of(device * depth + offset, 16), size)

    made = [[] for _ in range(SPLIT)]
    for number in range(SPLIT):
        unit = SPLIT * expert + (number ^ part)

        def add(source, target, number=number):
            copy = pltpu.make_async_copy(source, target, sems.at[number, len(made[number])])
            made[number].append(copy)

        for ref, device in ((own_ref, here), (near_ref, here ^ 1)):
            add(
                ref.at[unit, :, pl.ds(chip_first, slab)],
                weight.at[number, rows(device, 0, depth), :],
            )
        for at in range(2):
            moved = moved_refs[2 * number + at]
            moved_rows = pl.ds(offsets[2 * number + at], upper)
            for half in range(2):
                add(
                    moved.at[moved_rows, pl.ds(half * main, main)],
                    weight.at[
                        number,
                        rows(here ^ (2 + at), half * upper, upper),
                        pl.ds(pl.multiple_of(core * lanes, 128), main),
                    ],
                )
            add(moved.at[moved_rows, pl.ds(2 * main, lanes)], rest.at[number, at])
        add(b_ref.at[unit], bias.at[number])
        add(
            out_w_ref.at[unit],
            out_weight.at[number, pl.ds(pl.multiple_of(core * skip, 16), columns), :],
        )

    spare_sem = sems.shape[1] - sources
    x_copies = [
        pltpu.make_async_copy(
            x_ref.at[pl.ds(2 * per * (expert // 2), 2 * per), :],
            x_pairs.at[at],
            sems.at[0, spare_sem + at],
        )
        for at, x_ref in enumerate(x_refs)
    ]
    for copy in x_copies + made[0] + made[1]:
        copy.start()
    for number in range(SPLIT):
        spare = pl.ds(pl.multiple_of((1 - core) * columns, 16), skip)
        out_weight[number, spare, :] = jnp.zeros((skip, width), out_weight.dtype)
    for at, copy in enumerate(x_copies):
        copy.wait()
        pair = x_pairs[at].astype(jnp.float32)
        own_rows = pair[per * (expert % 2) : per * (expert % 2 + 1), :]
        total[per * at : per * (at + 1), :] = own_rows
    x_held[...] = total[...].astype(jnp.bfloat16)

    for number in range(SPLIT):
        for copy in made[number][:-1]:
            copy.wait()
        for at in range(2):
            tile = rest[number, at]
            turned = halves_turned(tile)
            for half in range(2):
                at_rows = rows(here ^ (2 + at), half * upper, upper)
                value = jnp.where(core == half, tile, turned)
                tail = pl.ds(pl.multiple_of((1 - core) * main, 128), lanes)
                weight[number, at_rows, tail] = value
        pre = jnp.dot(x_held[...], weight[number], preferred_element_type=jnp.float32)
        hidden = jax.nn.gelu(pre + bias[number], approximate=True).astype(jnp.bfloat16)
        made[number][-1].wait()
        piece = jnp.dot(hidden, out_weight[number], preferred_element_type=jnp.float32)
        total[...] = piece if number == 0 else total[...] + piece

    members = half_rows // (2 * CAP)
    for member in range(members):
        at = 2 * CAP * member
        keep_ref[CAP * member : CAP * (member + 1), :] = total[at : at + CAP, :]
        keep_far_ref[CAP * member : CAP * (member + 1), :] = total[at + CAP : at + 2 * CAP, :]
    given = [
        total[at : at + CAP, :]
        for image in range(2)
        for at in range(half_rows + CAP * image, 2 * half_rows, 2 * CAP)
    ]
    for number, rows_of in enumerate(given):
        total[CAP * number : CAP * (number + 1), :] = rows_of
    send_ref[...] = total[:half_rows, :].astype(jnp.bfloat16)


def expert_call(expert, xs, own, b, w_out, near, moved, events):
    width = w_out.shape[2]
    per = 2 * CAP
    half_rows = per * len(xs) // 2
    depth = own.shape[1]
    columns = w_out.shape[1]
    slab = b.shape[2]
    anywhere = pl.BlockSpec(memory_space=pl.ANY)

    return pl.pallas_call(
        functools.partial(
            expert_kernel, expert, len(xs), [offset for _, offset in moved], len(events)
        ),
        in_specs=[anywhere] * (4 + len(xs) + len(moved) + len(events)),
        out_specs=[pl.BlockSpec(memory_space=pltpu.VMEM)] * 3,
        scratch_shapes=[
            pltpu.VMEM((len(xs), 2 * per, width), jnp.bfloat16),
            pltpu.VMEM((2 * half_rows, width), jnp.bfloat16),
            pltpu.VMEM((SPLIT, width, slab), jnp.bfloat16),
            pltpu.VMEM((SPLIT, 2, depth // 2, 128), jnp.bfloat16),
            pltpu.VMEM((SPLIT, 1, slab), jnp.float32),
            pltpu.VMEM((SPLIT, slab, width), jnp.bfloat16),
            pltpu.VMEM((2 * half_rows, width), jnp.float32),
            pltpu.SemaphoreType.DMA((SPLIT, 10 + len(xs))),
        ],
        out_shape=[
            jax.ShapeDtypeStruct((half_rows // 2, width), jnp.float32),
            jax.ShapeDtypeStruct((half_rows // 2, width), jnp.float32),
            jax.ShapeDtypeStruct((half_rows, width), jnp.bfloat16),
        ],
        compiler_params=pltpu.CompilerParams(vmem_limit_bytes=54 << 20),
        cost_estimate=pl.CostEstimate(
            flops=2 * SPLIT * 2 * 2 * half_rows * width * columns,
            bytes_accessed=3 * (2 * SPLIT * 2 * width * columns + 16 * half_rows * width),
            transcendentals=SPLIT * 2 * half_rows * columns,
        ),
        name="expert",
    )(own, b, w_out, *xs, near, *[held for held, _ in moved], *events)


def combine_kernel(experts, group, last, route_ref, *refs):
    refs, held = refs[:-1], refs[-1]
    refs, out_ref = refs[:-1], refs[-1]
    before_ref = None
    if last:
        (before_ref, tokens_ref, settings_ref), refs = refs[:3], refs[3:]
    count = route_ref.shape[0]
    members = len(refs)
    size = len(group) * CAP
    for at, reply in enumerate(refs):
        held[at * size : (at + 1) * size, :] = reply[...].astype(jnp.float32)
    rows = held[...].astype(jnp.bfloat16)
    place = lax.broadcasted_iota(jnp.int32, (count, members * size), 1).astype(jnp.float32)
    row = lax.axis_index("ep")
    branch = before_ref[...] if last else None
    for k in range(2):
        expert, slot = route_ref[:, k : k + 1], route_ref[:, 2 + k : 3 + k]
        at = jnp.full_like(expert, -1.0)
        for ring in range(members):
            first = (row ^ ring) * experts + group[0]
            local = expert - first.astype(jnp.float32)
            inside = (local >= 0) & (local < len(group))
            at = jnp.where(inside, ring * size + local * CAP + slot, at)
        select = jnp.where(place == at, 1.0, 0.0).astype(jnp.bfloat16)
        term = route_ref[:, 4 + k : 5 + k] * jnp.dot(
            select, rows, preferred_element_type=jnp.float32
        )
        branch = term if branch is None else branch + term
    if last:
        tokens = tokens_ref[0].astype(jnp.float32)
        out_ref[0] = (tokens + settings_ref[2:3, :] * branch).astype(out_ref.dtype)
    else:
        out_ref[...] = branch


def combine_call(experts, group, route, replies, final=None):
    width = replies[0].shape[1]
    out = jax.ShapeDtypeStruct((route.shape[0], width), jnp.float32)
    if final:
        out = jax.ShapeDtypeStruct(final[1].shape, final[1].dtype)
    return pl.pallas_call(
        functools.partial(combine_kernel, experts, group, bool(final)),
        out_shape=out,
        scratch_shapes=[pltpu.VMEM((len(replies) * len(group) * CAP, width), jnp.float32)],
        name="combine",
    )(route, *(final or ()), *replies)


def recut_weights(hidden_states, expert_ids, modulation, router_weight, w_in, b_in, w_out):
    units, depth, _ = w_in.shape
    columns = w_out.shape[1]
    wide = 2 * columns
    experts = units // SPLIT
    members = lax.axis_size("ep")
    here = lax.axis_index("fs")
    core, chip = here & 1, here >> 1
    settings = modulation[0]

    def over(held, *events):
        return crossed(after(held, *events), "fs", 1)

    def beside(held, *events):
        return crossed(after(held, *events), "parts", 1)

    slab = -(-columns // 128) * 128
    own_b = lax.dynamic_slice(
        b_in, (0, chip * wide + core * (wide - slab)), (units, slab)
    )[:, None, :]
    place = np.arange(experts * 2 * CAP)
    image = place // CAP % 2
    wanted = np.where(
        image[:, None] == np.arange(2), (place // (2 * CAP) * CAP + place % CAP)[:, None], -np.inf
    ).astype(np.float32)

    ids = expert_ids[0].T.astype(jnp.float32)
    block = prepare_call(hidden_states, ids, settings)
    gate = after(here, block)
    near = over(w_in)
    opposite = crossed(after(block, gate), "fs", 2)
    upper = depth // 2
    fetched = ((0,), tuple(range(1, experts - 1)), (experts - 1,))
    cuts = cut_call(after(w_in, gate), wide, fetched)

    def fetch(number, *events):
        return crossed(after(cuts[number], *events), "fs", 2 + number % 2)

    def exchange(number, gate):
        size = len(fetched[number // 2])
        blocks = [far[number][at * upper : (at + 1) * upper] for at in range(size)]
        return [beside(held, gate) for held in blocks]

    def run(expert, *events):
        group = [expert in held for held in fetched].index(True)
        at = fetched[group].index(expert)
        moved = [(far[2 * group + k], at * upper) for k in range(2)]
        moved += [(other[2 * group + k][at], 0) for k in range(2)]
        return expert_call(expert, arrived + across, w_in, own_b, w_out, near, moved, events)

    far, other, outs = [fetch(0), fetch(1)], [], []
    opposite, near = lax.optimization_barrier((opposite, near))
    sending = dispatch_call(jnp.asarray(wanted), [block, opposite], members)
    arrived = [sending[0], crossed(sending[1], "ep", 1), crossed(sending[2], "ep", 2)]
    far.append(fetch(2, opposite))
    gate = after(gate, far[0], far[1], near)

    far.append(fetch(3, gate))
    other += [exchange(0, gate), exchange(1, gate)]
    gate = after(gate, far[2], *other[0], *other[1], arrived[1], arrived[2])

    far.append(fetch(4, gate))
    other.append(exchange(2, gate))
    arrived.append(crossed(after(sending[3], gate), "ep", 3))
    gate = after(gate, far[3], *other[2])

    far.append(fetch(5, gate))
    other.append(exchange(3, gate))
    gate = after(gate, far[4], arrived[3])

    other.append(exchange(4, gate))
    across = [over(held, gate) for held in arrived]
    route = route_call(block, router_weight)
    outs.append(run(0, route))
    gate = after(gate, far[5], *other[3])
    other.append(exchange(5, gate))
    half_rows = members * CAP

    def give(expert):
        held = outs[expert][1] + sent[expert][half_rows:].astype(jnp.float32)
        return crossed(held.astype(jnp.bfloat16), "fs", 2)

    sent = [over(outs[0][2])]
    outs.append(run(1, outs[0][0]))
    sent.append(over(outs[1][2]))
    given = [give(0), give(1)]
    outs.append(run(2, *sent))
    sent.append(over(outs[2][2]))
    given.append(give(2))
    outs.append(run(3, *given[:2]))
    sent.append(over(outs[3][2]))
    given.append(give(3))

    branch = None
    for group in (tuple(range(experts // 2)), tuple(range(experts // 2, experts))):
        wholes = []
        for e in group:
            half = outs[e][0] + sent[e][:half_rows].astype(jnp.float32)
            wholes.append((half + given[e].astype(jnp.float32)).astype(jnp.bfloat16))
        replies = []
        for d in range(members):
            reply = jnp.concatenate([held[d * CAP : (d + 1) * CAP] for held in wholes])
            replies.append(crossed(after(reply, sent[3]), "ep", d) if d else reply)
        if not group[0]:
            branch = combine_call(experts, group, route, replies)
        else:
            final = (branch, hidden_states, settings)
            branch = combine_call(experts, group, route, replies, final)
    return branch


def local(*arrays):
    w_in = arrays[4]
    recut = lax.axis_size("fs") == lax.axis_size("ep") == 4 and lax.axis_size("parts") == 2
    recut = recut and w_in.shape[0] == 4 * SPLIT and arrays[6].shape[1] % 128 == 64
    return (recut_weights if recut else gathered_weights)(*arrays)


def solution(mesh):
    placed = (
        P(("parts", "fs"), "ep", None),
        P(("parts", "fs"), "ep", None),
        P(("parts", "fs"), None, None),
        P(),
        P("ep", "fs", None),
        P("ep", None),
        P("ep", "fs", None),
    )
    return jax.shard_map(
        local, mesh=mesh, in_specs=placed, out_specs=P(("parts", "fs"), "ep", None), check_vma=False
    )
```

```python
import functools

import jax
import jax.numpy as jnp
import numpy as np
from jax import lax
from jax.experimental import pallas as pl
from jax.experimental.pallas import tpu as pltpu
from jax.sharding import PartitionSpec as P

EXPERTS = 16
SPLIT = 2
CAP = 20


norm_eps = 1e-06


def swapped(block, axis, distance):
    count = lax.axis_size(axis)
    route = []
    for low in range(count):
        high = low | 1 << distance
        if high != low and high < count:
            route += [(low, high), (high, low)]
    return lax.ppermute(block, axis, route)


def modulate(tokens, shift, scale):
    values = tokens.astype(jnp.float32)
    center = jnp.mean(values, axis=-1, keepdims=True)
    spread = jnp.mean(jnp.square(values - center), axis=-1, keepdims=True)
    normal = (values - center) * lax.rsqrt(spread + norm_eps)
    return (normal * (1.0 + scale) + shift).astype(jnp.bfloat16)


def slot_index(block_ids):
    flat_ids = block_ids.reshape(-1)
    one_hot = (flat_ids[:, None] == jnp.arange(EXPERTS, dtype=jnp.int32)[None, :]).astype(jnp.int32)
    earlier = jnp.cumsum(one_hot, axis=0, dtype=jnp.int32) - one_hot
    slots = jnp.sum(earlier * one_hot, axis=1, dtype=jnp.int32)
    return (flat_ids * CAP + slots).reshape(block_ids.shape)


def dispatch_rows(normed, flat_index):
    targets = jnp.arange(EXPERTS * CAP, dtype=jnp.int32)
    select = jnp.sum(
        (flat_index[None, :, :] == targets[:, None, None]).astype(jnp.int32),
        axis=2,
        dtype=jnp.int32,
    )
    return jnp.dot(select.astype(jnp.bfloat16), normed, preferred_element_type=jnp.float32).astype(
        jnp.bfloat16
    )


def combine(tokens, normed, gate_row, router_weight, block_ids, flat_index, expert_out):
    logits = jnp.dot(normed, router_weight, preferred_element_type=jnp.float32)
    picked = jnp.take_along_axis(logits, block_ids, axis=1)
    gap = picked[:, 0:1] - picked[:, 1:2]
    first = jnp.take(expert_out, flat_index[:, 0], axis=0).astype(jnp.float32)
    second = jnp.take(expert_out, flat_index[:, 1], axis=0).astype(jnp.float32)
    branch = jax.nn.sigmoid(gap) * first + jax.nn.sigmoid(-gap) * second
    return (tokens.astype(jnp.float32) + gate_row[None, :] * branch).astype(jnp.bfloat16)


def expert_compute(incoming, w_in, b_in, w_out):
    columns = incoming
    pre_act = jnp.einsum(
        "urd,udf->urf",
        columns,
        lax.all_gather(w_in, "fs", axis=1, tiled=True),
        preferred_element_type=jnp.float32,
    )
    hidden = jax.nn.gelu(pre_act + b_in[:, None, :], approximate=True).astype(jnp.bfloat16)
    columns = hidden
    produced = jnp.einsum(
        "urf,ufd->urd",
        columns,
        lax.all_gather(w_out, "fs", axis=1, tiled=True),
        preferred_element_type=jnp.float32,
    )
    return produced.astype(jnp.bfloat16)


def gathered_weights(
    hidden_states, expert_ids, modulation, router_weight, w_in, b_in, w_out
):
    token_count = hidden_states.shape[1]
    width = hidden_states.shape[2]
    tokens = hidden_states.reshape(token_count, width)
    block_ids = expert_ids.reshape(token_count, 2)
    settings = modulation[0]
    normed = modulate(tokens, settings[0][None, :], settings[1][None, :])
    flat_index = slot_index(block_ids)
    outgoing = dispatch_rows(normed, flat_index)
    per_expert = outgoing.reshape(EXPERTS, CAP, width)
    members = lax.axis_size("ep")
    local_units = w_in.shape[0]
    paired = local_units == 1
    half_cap = CAP // 2
    if paired:
        sending = per_expert.reshape(members, half_cap, width)
    else:
        sending = per_expert
    received = lax.all_to_all(sending, "ep", split_axis=0, concat_axis=1, tiled=True)
    if paired:
        parity = lax.axis_index("ep") % 2
        partner = swapped(received, "ep", 0)
        own_blocks = received.reshape(members, half_cap, width)
        other_blocks = partner.reshape(members, half_cap, width)
        lower = jnp.where(parity == 0, own_blocks, other_blocks)
        upper = jnp.where(parity == 0, other_blocks, own_blocks)
        incoming = jnp.stack([lower, upper], axis=1).reshape(1, members * CAP, width)
    else:
        incoming = jnp.repeat(received, SPLIT, axis=0)
    produced = expert_compute(incoming, w_in, b_in, w_out)
    if paired:
        halves = produced.reshape(members, 2, half_cap, width)
        kept_rows = jnp.where(parity == 0, halves[:, 0], halves[:, 1])
        given_rows = jnp.where(parity == 0, halves[:, 1], halves[:, 0])
        partner_out = swapped(given_rows, "ep", 0)
        reply = (kept_rows.astype(jnp.float32) + partner_out.astype(jnp.float32)).astype(
            jnp.bfloat16
        )
    else:
        local_experts = local_units // SPLIT
        summed = jnp.sum(
            produced.astype(jnp.float32).reshape(local_experts, SPLIT, members, CAP, width), axis=1
        )
        reply = (
            summed.astype(jnp.bfloat16)
            .transpose(1, 0, 2, 3)
            .reshape(members, local_experts * CAP, width)
        )
    returned = lax.all_to_all(reply, "ep", split_axis=0, concat_axis=0, tiled=True)
    expert_out = returned.reshape(EXPERTS, CAP, width)
    result = combine(
        tokens,
        normed,
        settings[2],
        router_weight,
        block_ids,
        flat_index,
        expert_out.reshape(EXPERTS * CAP, width),
    )
    return result.reshape(1, token_count, width)


def crossed(block, axis, mask):
    count = lax.axis_size(axis)
    return lax.ppermute(block, axis, [(i, i ^ mask) for i in range(count)])


def after(value, *events):
    return lax.optimization_barrier((value, *events))[0] if events else value


def slot_rows(ids, experts_count):
    tokens = ids[0].shape[1]
    experts = lax.broadcasted_iota(jnp.int32, (experts_count, tokens), 0).astype(jnp.float32)
    chosen = [jnp.where(experts == row, 1.0, 0.0) for row in ids]
    earlier = jnp.where(
        lax.broadcasted_iota(jnp.int32, (tokens, tokens), 0)
        < lax.broadcasted_iota(jnp.int32, (tokens, tokens), 1),
        1.0,
        0.0,
    )
    before = jnp.dot(
        (chosen[0] + chosen[1]).astype(jnp.bfloat16),
        earlier.astype(jnp.bfloat16),
        preferred_element_type=jnp.float32,
    )
    return [jnp.sum(before * one, axis=0, keepdims=True) for one in chosen]


def prepare_kernel(tokens_ref, ids_ref, settings_ref, out_ref):
    count, width = tokens_ref.shape[1:]
    out_ref[:count, :] = modulate(tokens_ref[0], settings_ref[0:1, :], settings_ref[1:2, :])
    ids = [ids_ref[0:1, :], ids_ref[1:2, :]]
    listed = [*ids, *slot_rows(ids, EXPERTS), jnp.zeros((1, width - 4 * count), jnp.float32)]
    row = jnp.concatenate(listed, axis=1)
    first = lax.broadcasted_iota(jnp.int32, (16, width), 0) == 0
    out_ref[count:, :] = jnp.where(first, row, 0.0).astype(jnp.bfloat16)


def prepare_call(hidden_states, ids, settings):
    count, width = hidden_states.shape[1:]
    return pl.pallas_call(
        prepare_kernel,
        out_shape=jax.ShapeDtypeStruct((count + 16, width), jnp.bfloat16),
        name="prepare",
    )(hidden_states, ids, settings)


def route_kernel(block_ref, router_ref, out_ref):
    count = out_ref.shape[0]
    listed = block_ref[count:, :].astype(jnp.float32)[0:1, :]
    place = lax.broadcasted_iota(jnp.int32, (count, count), 0)
    spread = jnp.zeros((count, count), jnp.float32)
    for k in range(4):
        spread = jnp.where(place == k, listed[:, k * count : (k + 1) * count], spread)
    columns = spread.T
    logits = jnp.dot(block_ref[:count, :], router_ref[...], preferred_element_type=jnp.float32)
    experts = lax.broadcasted_iota(jnp.int32, logits.shape, 1).astype(jnp.float32)
    picked = [
        jnp.sum(jnp.where(experts == columns[:, k : k + 1], logits, 0.0), axis=1, keepdims=True)
        for k in range(2)
    ]
    gap = picked[0] - picked[1]
    lanes = lax.broadcasted_iota(jnp.int32, (count, count), 1)
    columns = jnp.where(lanes == 4, jax.nn.sigmoid(gap), columns)
    out_ref[...] = jnp.where(lanes == 5, jax.nn.sigmoid(-gap), columns)


def route_call(block, router_weight):
    count = block.shape[0] - 16
    return pl.pallas_call(
        route_kernel,
        out_shape=jax.ShapeDtypeStruct((count, count), jnp.float32),
        name="route",
    )(block, router_weight)


def dispatch_kernel(wanted_ref, *refs):
    rows, images = wanted_ref.shape
    blocks, outs = refs[:images], refs[images:]
    count = blocks[0].shape[0] - 16
    places = []
    for block in blocks:
        listed = block[count:, :].astype(jnp.float32)[0:1, :]
        parts = [listed[:, k * count : (k + 1) * count] for k in range(4)]
        places.append([parts[k] * CAP + parts[2 + k] for k in range(2)])
    tokens = jnp.concatenate([block[:count, :] for block in blocks], axis=0)
    owner = lax.axis_index("ep")
    for number, out_ref in enumerate(outs):
        first = (owner ^ number) * (rows // images)
        choices = []
        for image in range(images):
            wanted = wanted_ref[:, image : image + 1] + first.astype(jnp.float32)
            match = (wanted == places[image][0]) | (wanted == places[image][1])
            choices.append(jnp.where(match, 1.0, 0.0).astype(jnp.bfloat16))
        out_ref[...] = jnp.dot(
            jnp.concatenate(choices, axis=1), tokens, preferred_element_type=jnp.float32
        ).astype(jnp.bfloat16)


def dispatch_call(wanted, blocks, members):
    rows = wanted.shape[0]
    width = blocks[0].shape[1]
    return pl.pallas_call(
        dispatch_kernel,
        out_shape=[jax.ShapeDtypeStruct((rows, width), jnp.bfloat16)] * members,
        cost_estimate=pl.CostEstimate(
            flops=2 * members * rows * len(blocks) * blocks[0].shape[0] * width,
            bytes_accessed=4 * members * rows * width,
            transcendentals=0,
        ),
        name="dispatch",
    )(wanted, *blocks)


def halves_turned(tile):
    half = tile.shape[1] // 2
    return pltpu.roll(tile.astype(jnp.float32), half, 1).astype(tile.dtype)


def where_am_i():
    here, part = lax.axis_index("fs"), lax.axis_index("parts")
    return here, part, here & 1


def cut_kernel(groups, w_in_ref, *refs):
    outs, (held, tiles, sems) = refs[:-3], refs[-3:]
    experts, depth, lanes = tiles.shape
    upper = depth // 2
    slots = [(g, at) for g, group in enumerate(groups) for at in range(len(group))]
    wide = held.shape[2]
    main = (wide - lanes) // 2
    here, part, core = where_am_i()
    chip = here >> 1
    first = (1 - chip) * wide
    rest = [
        pltpu.make_async_copy(
            w_in_ref.at[SPLIT * e + part, :, pl.ds(pl.multiple_of(first + main, 128), lanes)],
            tiles.at[e],
            sems.at[0, e],
        )
        for e in range(experts)
    ]
    arriving, leaving = [], []
    for number in range(2 * experts):
        e, target = number // 2, core ^ (number % 2)
        group, at = slots[e]
        out = outs[2 * group + number % 2].at[pl.ds(at * upper, upper), :]
        columns = pl.ds(pl.multiple_of(first + target * (main + lanes), 128), main)
        arriving.append(
            [
                pltpu.make_async_copy(
                    w_in_ref.at[SPLIT * e + part, pl.ds(half * upper, upper), columns],
                    held.at[number, :, pl.ds(half * main, main)],
                    sems.at[1 + half, number],
                )
                for half in range(2)
            ]
        )
        leaving.append(pltpu.make_async_copy(held.at[number], out, sems.at[3, number]))
    for copy in rest:
        copy.start()
    for halves in arriving:
        for copy in halves:
            copy.start()
    left = lax.broadcasted_iota(jnp.int32, (upper, lanes), 1) < lanes // 2
    for number, halves in enumerate(arriving):
        e, target = number // 2, core ^ (number % 2)
        if number % 2 == 0:
            rest[e].wait()
        top, bottom = tiles[e, :upper, :], tiles[e, upper:, :]
        low = jnp.where(left, top, halves_turned(bottom))
        high = jnp.where(left, halves_turned(top), bottom)
        held[number, :, 2 * main :] = jnp.where(target == 0, low, high)
        for copy in halves:
            copy.wait()
        leaving[number].start()
    for copy in leaving:
        copy.wait()


def cut_call(w_in, wide, groups):
    units, depth, _ = w_in.shape
    experts = units // SPLIT
    anywhere = pl.BlockSpec(memory_space=pl.ANY)
    blocks = 2 * experts
    return pl.pallas_call(
        functools.partial(cut_kernel, groups),
        in_specs=[anywhere],
        out_specs=[anywhere] * (2 * len(groups)),
        out_shape=[
            jax.ShapeDtypeStruct((len(group) * (depth // 2), wide), jnp.bfloat16)
            for group in groups
            for _ in range(2)
        ],
        scratch_shapes=[
            pltpu.VMEM((blocks, depth // 2, wide), jnp.bfloat16),
            pltpu.VMEM((experts, depth, 128), jnp.bfloat16),
            pltpu.SemaphoreType.DMA((4, blocks)),
        ],
        compiler_params=pltpu.CompilerParams(vmem_limit_bytes=60 << 20),
        cost_estimate=pl.CostEstimate(
            flops=0, bytes_accessed=4 * blocks * (depth // 2) * wide, transcendentals=0
        ),
        name="cut",
    )(w_in)


def expert_kernel(expert, sources, offsets, events, own_ref, b_ref, out_w_ref, *refs):
    x_refs, refs = refs[:sources], refs[sources:]
    near_ref, moved_refs, refs = refs[0], refs[1:5], refs[5 + events :]
    keep_ref, keep_far_ref, send_ref, *refs = refs
    x_pairs, x_held, weight, rest, bias, out_weight, total, sems = refs
    here, part, core = where_am_i()
    depth = own_ref.shape[1]
    columns, width = out_w_ref.shape[1:]
    upper, lanes = rest.shape[2:]
    slab = weight.shape[2]
    skip = slab - columns
    wide = 2 * columns
    main = slab - lanes
    chip_first = pl.multiple_of((here >> 1) * wide + core * (wide - slab), 128)
    half_rows = x_held.shape[0] // 2
    per = x_pairs.shape[1] // 2

    def rows(device, offset, size):
        return pl.ds(pl.multiple_of(device * depth + offset, 16), size)

    made = [[] for _ in range(SPLIT)]
    for number in range(SPLIT):
        unit = SPLIT * expert + (number ^ part)

        def add(source, target, number=number):
            copy = pltpu.make_async_copy(source, target, sems.at[number, len(made[number])])
            made[number].append(copy)

        for ref, device in ((own_ref, here), (near_ref, here ^ 1)):
            add(
                ref.at[unit, :, pl.ds(chip_first, slab)],
                weight.at[number, rows(device, 0, depth), :],
            )
        for at in range(2):
            moved = moved_refs[2 * number + at]
            moved_rows = pl.ds(offsets[2 * number + at], upper)
            for half in range(2):
                add(
                    moved.at[moved_rows, pl.ds(half * main, main)],
                    weight.at[
                        number,
                        rows(here ^ (2 + at), half * upper, upper),
                        pl.ds(pl.multiple_of(core * lanes, 128), main),
                    ],
                )
            add(moved.at[moved_rows, pl.ds(2 * main, lanes)], rest.at[number, at])
        add(b_ref.at[unit], bias.at[number])
        add(
            out_w_ref.at[unit],
            out_weight.at[number, pl.ds(pl.multiple_of(core * skip, 16), columns), :],
        )

    spare_sem = sems.shape[1] - sources
    x_copies = [
        pltpu.make_async_copy(
            x_ref.at[pl.ds(2 * per * (expert // 2), 2 * per), :],
            x_pairs.at[at],
            sems.at[0, spare_sem + at],
        )
        for at, x_ref in enumerate(x_refs)
    ]
    for copy in x_copies + made[0] + made[1]:
        copy.start()
    for number in range(SPLIT):
        spare = pl.ds(pl.multiple_of((1 - core) * columns, 16), skip)
        out_weight[number, spare, :] = jnp.zeros((skip, width), out_weight.dtype)
    for at, copy in enumerate(x_copies):
        copy.wait()
        pair = x_pairs[at].astype(jnp.float32)
        own_rows = pair[per * (expert % 2) : per * (expert % 2 + 1), :]
        total[per * at : per * (at + 1), :] = own_rows
    x_held[...] = total[...].astype(jnp.bfloat16)

    for number in range(SPLIT):
        for copy in made[number][:-1]:
            copy.wait()
        for at in range(2):
            tile = rest[number, at]
            turned = halves_turned(tile)
            for half in range(2):
                at_rows = rows(here ^ (2 + at), half * upper, upper)
                value = jnp.where(core == half, tile, turned)
                tail = pl.ds(pl.multiple_of((1 - core) * main, 128), lanes)
                weight[number, at_rows, tail] = value
        pre = jnp.dot(x_held[...], weight[number], preferred_element_type=jnp.float32)
        hidden = jax.nn.gelu(pre + bias[number], approximate=True).astype(jnp.bfloat16)
        made[number][-1].wait()
        piece = jnp.dot(hidden, out_weight[number], preferred_element_type=jnp.float32)
        total[...] = piece if number == 0 else total[...] + piece

    members = half_rows // (2 * CAP)
    for member in range(members):
        at = 2 * CAP * member
        keep_ref[CAP * member : CAP * (member + 1), :] = total[at : at + CAP, :]
        keep_far_ref[CAP * member : CAP * (member + 1), :] = total[at + CAP : at + 2 * CAP, :]
    given = [
        total[at : at + CAP, :]
        for image in range(2)
        for at in range(half_rows + CAP * image, 2 * half_rows, 2 * CAP)
    ]
    for number, rows_of in enumerate(given):
        total[CAP * number : CAP * (number + 1), :] = rows_of
    send_ref[...] = total[:half_rows, :].astype(jnp.bfloat16)


def expert_call(expert, xs, own, b, w_out, near, moved, events):
    width = w_out.shape[2]
    per = 2 * CAP
    half_rows = per * len(xs) // 2
    depth = own.shape[1]
    columns = w_out.shape[1]
    slab = b.shape[2]
    anywhere = pl.BlockSpec(memory_space=pl.ANY)

    return pl.pallas_call(
        functools.partial(
            expert_kernel, expert, len(xs), [offset for _, offset in moved], len(events)
        ),
        in_specs=[anywhere] * (4 + len(xs) + len(moved) + len(events)),
        out_specs=[pl.BlockSpec(memory_space=pltpu.VMEM)] * 3,
        scratch_shapes=[
            pltpu.VMEM((len(xs), 2 * per, width), jnp.bfloat16),
            pltpu.VMEM((2 * half_rows, width), jnp.bfloat16),
            pltpu.VMEM((SPLIT, width, slab), jnp.bfloat16),
            pltpu.VMEM((SPLIT, 2, depth // 2, 128), jnp.bfloat16),
            pltpu.VMEM((SPLIT, 1, slab), jnp.float32),
            pltpu.VMEM((SPLIT, slab, width), jnp.bfloat16),
            pltpu.VMEM((2 * half_rows, width), jnp.float32),
            pltpu.SemaphoreType.DMA((SPLIT, 10 + len(xs))),
        ],
        out_shape=[
            jax.ShapeDtypeStruct((half_rows // 2, width), jnp.float32),
            jax.ShapeDtypeStruct((half_rows // 2, width), jnp.float32),
            jax.ShapeDtypeStruct((half_rows, width), jnp.bfloat16),
        ],
        compiler_params=pltpu.CompilerParams(vmem_limit_bytes=54 << 20),
        cost_estimate=pl.CostEstimate(
            flops=2 * SPLIT * 2 * 2 * half_rows * width * columns,
            bytes_accessed=3 * (2 * SPLIT * 2 * width * columns + 16 * half_rows * width),
            transcendentals=SPLIT * 2 * half_rows * columns,
        ),
        name="expert",
    )(own, b, w_out, *xs, near, *[held for held, _ in moved], *events)


def combine_kernel(experts, group, last, route_ref, *refs):
    refs, held = refs[:-1], refs[-1]
    refs, out_ref = refs[:-1], refs[-1]
    before_ref = None
    if last:
        (before_ref, tokens_ref, settings_ref), refs = refs[:3], refs[3:]
    count = route_ref.shape[0]
    members = len(refs)
    size = len(group) * CAP
    for at, reply in enumerate(refs):
        held[at * size : (at + 1) * size, :] = reply[...].astype(jnp.float32)
    rows = held[...].astype(jnp.bfloat16)
    place = lax.broadcasted_iota(jnp.int32, (count, members * size), 1).astype(jnp.float32)
    row = lax.axis_index("ep")
    branch = before_ref[...] if last else None
    for k in range(2):
        expert, slot = route_ref[:, k : k + 1], route_ref[:, 2 + k : 3 + k]
        at = jnp.full_like(expert, -1.0)
        for ring in range(members):
            first = (row ^ ring) * experts + group[0]
            local = expert - first.astype(jnp.float32)
            inside = (local >= 0) & (local < len(group))
            at = jnp.where(inside, ring * size + local * CAP + slot, at)
        select = jnp.where(place == at, 1.0, 0.0).astype(jnp.bfloat16)
        term = route_ref[:, 4 + k : 5 + k] * jnp.dot(
            select, rows, preferred_element_type=jnp.float32
        )
        branch = term if branch is None else branch + term
    if last:
        tokens = tokens_ref[0].astype(jnp.float32)
        out_ref[0] = (tokens + settings_ref[2:3, :] * branch).astype(out_ref.dtype)
    else:
        out_ref[...] = branch


def combine_call(experts, group, route, replies, final=None):
    width = replies[0].shape[1]
    out = jax.ShapeDtypeStruct((route.shape[0], width), jnp.float32)
    if final:
        out = jax.ShapeDtypeStruct(final[1].shape, final[1].dtype)
    return pl.pallas_call(
        functools.partial(combine_kernel, experts, group, bool(final)),
        out_shape=out,
        scratch_shapes=[pltpu.VMEM((len(replies) * len(group) * CAP, width), jnp.float32)],
        name="combine",
    )(route, *(final or ()), *replies)


def recut_weights(hidden_states, expert_ids, modulation, router_weight, w_in, b_in, w_out):
    units, depth, _ = w_in.shape
    columns = w_out.shape[1]
    wide = 2 * columns
    experts = units // SPLIT
    members = lax.axis_size("ep")
    here = lax.axis_index("fs")
    core, chip = here & 1, here >> 1
    settings = modulation[0]

    def over(held, *events):
        return crossed(after(held, *events), "fs", 1)

    def beside(held, *events):
        return crossed(after(held, *events), "parts", 1)

    slab = -(-columns // 128) * 128
    own_b = lax.dynamic_slice(
        b_in, (0, chip * wide + core * (wide - slab)), (units, slab)
    )[:, None, :]
    place = np.arange(experts * 2 * CAP)
    image = place // CAP % 2
    wanted = np.where(
        image[:, None] == np.arange(2), (place // (2 * CAP) * CAP + place % CAP)[:, None], -np.inf
    ).astype(np.float32)

    ids = expert_ids[0].T.astype(jnp.float32)
    block = prepare_call(hidden_states, ids, settings)
    gate = after(here, block)
    near = over(w_in)
    opposite = crossed(after(block, gate), "fs", 2)
    upper = depth // 2
    fetched = ((0,), tuple(range(1, experts - 1)), (experts - 1,))
    cuts = cut_call(after(w_in, gate), wide, fetched)

    def fetch(number, *events):
        return crossed(after(cuts[number], *events), "fs", 2 + number % 2)

    def exchange(number, gate):
        size = len(fetched[number // 2])
        blocks = [far[number][at * upper : (at + 1) * upper] for at in range(size)]
        return [beside(held, gate) for held in blocks]

    def run(expert, *events):
        group = [expert in held for held in fetched].index(True)
        at = fetched[group].index(expert)
        moved = [(far[2 * group + k], at * upper) for k in range(2)]
        moved += [(other[2 * group + k][at], 0) for k in range(2)]
        return expert_call(expert, arrived + across, w_in, own_b, w_out, near, moved, events)

    far, other, outs = [fetch(0), fetch(1)], [], []
    opposite, near = lax.optimization_barrier((opposite, near))
    sending = dispatch_call(jnp.asarray(wanted), [block, opposite], members)
    arrived = [sending[0], crossed(sending[1], "ep", 1), crossed(sending[2], "ep", 2)]
    route = route_call(block, router_weight)
    far.append(fetch(2, opposite))
    gate = after(gate, far[0], far[1], near)

    far.append(fetch(3, gate))
    other += [exchange(0, gate), exchange(1, gate)]
    gate = after(gate, far[2], *other[0], *other[1], arrived[1], arrived[2])

    far.append(fetch(4, gate))
    other.append(exchange(2, gate))
    arrived.append(crossed(after(sending[3], gate, route, own_b), "ep", 3))
    gate = after(gate, far[3], *other[2])

    far.append(fetch(5, gate))
    other.append(exchange(3, gate))
    gate = after(gate, far[4], arrived[3])

    other.append(exchange(4, gate))
    across = [over(held, gate) for held in arrived]
    outs.append(run(0))
    gate = after(gate, far[5], *other[3])
    other.append(exchange(5, gate))
    half_rows = members * CAP

    def give(expert):
        held = outs[expert][1] + sent[expert][half_rows:].astype(jnp.float32)
        return crossed(held.astype(jnp.bfloat16), "fs", 2)

    sent = [over(outs[0][2])]
    outs.append(run(1, outs[0][0], far[5], other[3][1]))
    sent.append(over(outs[1][2]))
    given = [give(0), give(1)]
    outs.append(run(2, *sent))
    sent.append(over(outs[2][2]))
    given.append(give(2))
    outs.append(run(3, *given[:2]))
    sent.append(over(outs[3][2]))
    given.append(give(3))

    branch = None
    for group in (tuple(range(experts // 2)), tuple(range(experts // 2, experts))):
        wholes = []
        for e in group:
            half = outs[e][0] + sent[e][:half_rows].astype(jnp.float32)
            wholes.append((half + given[e].astype(jnp.float32)).astype(jnp.bfloat16))
        replies = []
        for d in range(members):
            reply = jnp.concatenate([held[d * CAP : (d + 1) * CAP] for held in wholes])
            replies.append(crossed(after(reply, sent[3]), "ep", d) if d else reply)
        if not group[0]:
            branch = combine_call(experts, group, route, replies)
        else:
            final = (branch, hidden_states, settings)
            branch = combine_call(experts, group, route, replies, final)
    return branch


def local(*arrays):
    w_in = arrays[4]
    recut = lax.axis_size("fs") == lax.axis_size("ep") == 4 and lax.axis_size("parts") == 2
    recut = recut and w_in.shape[0] == 4 * SPLIT and arrays[6].shape[1] % 128 == 64
    return (recut_weights if recut else gathered_weights)(*arrays)


def solution(mesh):
    placed = (
        P(("parts", "fs"), "ep", None),
        P(("parts", "fs"), "ep", None),
        P(("parts", "fs"), None, None),
        P(),
        P("ep", "fs", None),
        P("ep", None),
        P("ep", "fs", None),
    )
    return jax.shard_map(
        local, mesh=mesh, in_specs=placed, out_specs=P(("parts", "fs"), "ep", None), check_vma=False
    )
```

```python
import functools

import jax
import jax.numpy as jnp
import numpy as np
from jax import lax
from jax.experimental import pallas as pl
from jax.experimental.pallas import tpu as pltpu
from jax.sharding import PartitionSpec as P

EXPERTS = 16
SPLIT = 2
CAP = 20


norm_eps = 1e-06


def swapped(block, axis, distance):
    count = lax.axis_size(axis)
    route = []
    for low in range(count):
        high = low | 1 << distance
        if high != low and high < count:
            route += [(low, high), (high, low)]
    return lax.ppermute(block, axis, route)


def modulate(tokens, shift, scale):
    values = tokens.astype(jnp.float32)
    center = jnp.mean(values, axis=-1, keepdims=True)
    spread = jnp.mean(jnp.square(values - center), axis=-1, keepdims=True)
    normal = (values - center) * lax.rsqrt(spread + norm_eps)
    return (normal * (1.0 + scale) + shift).astype(jnp.bfloat16)


def slot_index(block_ids):
    flat_ids = block_ids.reshape(-1)
    one_hot = (flat_ids[:, None] == jnp.arange(EXPERTS, dtype=jnp.int32)[None, :]).astype(jnp.int32)
    earlier = jnp.cumsum(one_hot, axis=0, dtype=jnp.int32) - one_hot
    slots = jnp.sum(earlier * one_hot, axis=1, dtype=jnp.int32)
    return (flat_ids * CAP + slots).reshape(block_ids.shape)


def dispatch_rows(normed, flat_index):
    targets = jnp.arange(EXPERTS * CAP, dtype=jnp.int32)
    select = jnp.sum(
        (flat_index[None, :, :] == targets[:, None, None]).astype(jnp.int32),
        axis=2,
        dtype=jnp.int32,
    )
    return jnp.dot(select.astype(jnp.bfloat16), normed, preferred_element_type=jnp.float32).astype(
        jnp.bfloat16
    )


def combine(tokens, normed, gate_row, router_weight, block_ids, flat_index, expert_out):
    logits = jnp.dot(normed, router_weight, preferred_element_type=jnp.float32)
    picked = jnp.take_along_axis(logits, block_ids, axis=1)
    gap = picked[:, 0:1] - picked[:, 1:2]
    first = jnp.take(expert_out, flat_index[:, 0], axis=0).astype(jnp.float32)
    second = jnp.take(expert_out, flat_index[:, 1], axis=0).astype(jnp.float32)
    branch = jax.nn.sigmoid(gap) * first + jax.nn.sigmoid(-gap) * second
    return (tokens.astype(jnp.float32) + gate_row[None, :] * branch).astype(jnp.bfloat16)


def expert_compute(incoming, w_in, b_in, w_out):
    columns = incoming
    pre_act = jnp.einsum(
        "urd,udf->urf",
        columns,
        lax.all_gather(w_in, "fs", axis=1, tiled=True),
        preferred_element_type=jnp.float32,
    )
    hidden = jax.nn.gelu(pre_act + b_in[:, None, :], approximate=True).astype(jnp.bfloat16)
    columns = hidden
    produced = jnp.einsum(
        "urf,ufd->urd",
        columns,
        lax.all_gather(w_out, "fs", axis=1, tiled=True),
        preferred_element_type=jnp.float32,
    )
    return produced.astype(jnp.bfloat16)


def gathered_weights(
    hidden_states, expert_ids, modulation, router_weight, w_in, b_in, w_out
):
    token_count = hidden_states.shape[1]
    width = hidden_states.shape[2]
    tokens = hidden_states.reshape(token_count, width)
    block_ids = expert_ids.reshape(token_count, 2)
    settings = modulation[0]
    normed = modulate(tokens, settings[0][None, :], settings[1][None, :])
    flat_index = slot_index(block_ids)
    outgoing = dispatch_rows(normed, flat_index)
    per_expert = outgoing.reshape(EXPERTS, CAP, width)
    members = lax.axis_size("ep")
    local_units = w_in.shape[0]
    paired = local_units == 1
    half_cap = CAP // 2
    if paired:
        sending = per_expert.reshape(members, half_cap, width)
    else:
        sending = per_expert
    received = lax.all_to_all(sending, "ep", split_axis=0, concat_axis=1, tiled=True)
    if paired:
        parity = lax.axis_index("ep") % 2
        partner = swapped(received, "ep", 0)
        own_blocks = received.reshape(members, half_cap, width)
        other_blocks = partner.reshape(members, half_cap, width)
        lower = jnp.where(parity == 0, own_blocks, other_blocks)
        upper = jnp.where(parity == 0, other_blocks, own_blocks)
        incoming = jnp.stack([lower, upper], axis=1).reshape(1, members * CAP, width)
    else:
        incoming = jnp.repeat(received, SPLIT, axis=0)
    produced = expert_compute(incoming, w_in, b_in, w_out)
    if paired:
        halves = produced.reshape(members, 2, half_cap, width)
        kept_rows = jnp.where(parity == 0, halves[:, 0], halves[:, 1])
        given_rows = jnp.where(parity == 0, halves[:, 1], halves[:, 0])
        partner_out = swapped(given_rows, "ep", 0)
        reply = (kept_rows.astype(jnp.float32) + partner_out.astype(jnp.float32)).astype(
            jnp.bfloat16
        )
    else:
        local_experts = local_units // SPLIT
        summed = jnp.sum(
            produced.astype(jnp.float32).reshape(local_experts, SPLIT, members, CAP, width), axis=1
        )
        reply = (
            summed.astype(jnp.bfloat16)
            .transpose(1, 0, 2, 3)
            .reshape(members, local_experts * CAP, width)
        )
    returned = lax.all_to_all(reply, "ep", split_axis=0, concat_axis=0, tiled=True)
    expert_out = returned.reshape(EXPERTS, CAP, width)
    result = combine(
        tokens,
        normed,
        settings[2],
        router_weight,
        block_ids,
        flat_index,
        expert_out.reshape(EXPERTS * CAP, width),
    )
    return result.reshape(1, token_count, width)


def crossed(block, axis, mask):
    count = lax.axis_size(axis)
    return lax.ppermute(block, axis, [(i, i ^ mask) for i in range(count)])


def after(value, *events):
    return lax.optimization_barrier((value, *events))[0] if events else value


def slot_rows(ids, experts_count):
    tokens = ids[0].shape[1]
    experts = lax.broadcasted_iota(jnp.int32, (experts_count, tokens), 0).astype(jnp.float32)
    chosen = [jnp.where(experts == row, 1.0, 0.0) for row in ids]
    earlier = jnp.where(
        lax.broadcasted_iota(jnp.int32, (tokens, tokens), 0)
        < lax.broadcasted_iota(jnp.int32, (tokens, tokens), 1),
        1.0,
        0.0,
    )
    before = jnp.dot(
        (chosen[0] + chosen[1]).astype(jnp.bfloat16),
        earlier.astype(jnp.bfloat16),
        preferred_element_type=jnp.float32,
    )
    return [jnp.sum(before * one, axis=0, keepdims=True) for one in chosen]


def prepare_kernel(tokens_ref, ids_ref, settings_ref, out_ref):
    count, width = tokens_ref.shape[1:]
    out_ref[:count, :] = modulate(tokens_ref[0], settings_ref[0:1, :], settings_ref[1:2, :])
    ids = [ids_ref[0:1, :], ids_ref[1:2, :]]
    listed = [*ids, *slot_rows(ids, EXPERTS), jnp.zeros((1, width - 4 * count), jnp.float32)]
    row = jnp.concatenate(listed, axis=1)
    first = lax.broadcasted_iota(jnp.int32, (16, width), 0) == 0
    out_ref[count:, :] = jnp.where(first, row, 0.0).astype(jnp.bfloat16)


def prepare_call(hidden_states, ids, settings):
    count, width = hidden_states.shape[1:]
    return pl.pallas_call(
        prepare_kernel,
        out_shape=jax.ShapeDtypeStruct((count + 16, width), jnp.bfloat16),
        name="prepare",
    )(hidden_states, ids, settings)


def route_kernel(block_ref, router_ref, out_ref):
    count = out_ref.shape[0]
    listed = block_ref[count:, :].astype(jnp.float32)[0:1, :]
    place = lax.broadcasted_iota(jnp.int32, (count, count), 0)
    spread = jnp.zeros((count, count), jnp.float32)
    for k in range(4):
        spread = jnp.where(place == k, listed[:, k * count : (k + 1) * count], spread)
    columns = spread.T
    logits = jnp.dot(block_ref[:count, :], router_ref[...], preferred_element_type=jnp.float32)
    experts = lax.broadcasted_iota(jnp.int32, logits.shape, 1).astype(jnp.float32)
    picked = [
        jnp.sum(jnp.where(experts == columns[:, k : k + 1], logits, 0.0), axis=1, keepdims=True)
        for k in range(2)
    ]
    gap = picked[0] - picked[1]
    lanes = lax.broadcasted_iota(jnp.int32, (count, count), 1)
    columns = jnp.where(lanes == 4, jax.nn.sigmoid(gap), columns)
    out_ref[...] = jnp.where(lanes == 5, jax.nn.sigmoid(-gap), columns)


def route_call(block, router_weight):
    count = block.shape[0] - 16
    return pl.pallas_call(
        route_kernel,
        out_shape=jax.ShapeDtypeStruct((count, count), jnp.float32),
        name="route",
    )(block, router_weight)


def dispatch_kernel(wanted_ref, *refs):
    rows, images = wanted_ref.shape
    blocks, outs = refs[:images], refs[images:]
    count = blocks[0].shape[0] - 16
    places = []
    for block in blocks:
        listed = block[count:, :].astype(jnp.float32)[0:1, :]
        parts = [listed[:, k * count : (k + 1) * count] for k in range(4)]
        places.append([parts[k] * CAP + parts[2 + k] for k in range(2)])
    tokens = jnp.concatenate([block[:count, :] for block in blocks], axis=0)
    owner = lax.axis_index("ep")
    for number, out_ref in enumerate(outs):
        first = (owner ^ number) * (rows // images)
        choices = []
        for image in range(images):
            wanted = wanted_ref[:, image : image + 1] + first.astype(jnp.float32)
            match = (wanted == places[image][0]) | (wanted == places[image][1])
            choices.append(jnp.where(match, 1.0, 0.0).astype(jnp.bfloat16))
        out_ref[...] = jnp.dot(
            jnp.concatenate(choices, axis=1), tokens, preferred_element_type=jnp.float32
        ).astype(jnp.bfloat16)


def dispatch_call(wanted, blocks, members):
    rows = wanted.shape[0]
    width = blocks[0].shape[1]
    return pl.pallas_call(
        dispatch_kernel,
        out_shape=[jax.ShapeDtypeStruct((rows, width), jnp.bfloat16)] * members,
        cost_estimate=pl.CostEstimate(
            flops=2 * members * rows * len(blocks) * blocks[0].shape[0] * width,
            bytes_accessed=4 * members * rows * width,
            transcendentals=0,
        ),
        name="dispatch",
    )(wanted, *blocks)


def halves_turned(tile):
    half = tile.shape[1] // 2
    return pltpu.roll(tile.astype(jnp.float32), half, 1).astype(tile.dtype)


def where_am_i():
    here, part = lax.axis_index("fs"), lax.axis_index("parts")
    return here, part, here & 1


def cut_kernel(groups, w_in_ref, *refs):
    outs, (held, tiles, sems) = refs[:-3], refs[-3:]
    experts, depth, lanes = tiles.shape
    upper = depth // 2
    slots = [(g, at) for g, group in enumerate(groups) for at in range(len(group))]
    wide = held.shape[2]
    main = (wide - lanes) // 2
    here, part, core = where_am_i()
    chip = here >> 1
    first = (1 - chip) * wide
    rest = [
        pltpu.make_async_copy(
            w_in_ref.at[SPLIT * e + part, :, pl.ds(pl.multiple_of(first + main, 128), lanes)],
            tiles.at[e],
            sems.at[0, e],
        )
        for e in range(experts)
    ]
    arriving, leaving = [], []
    for number in range(2 * experts):
        e, target = number // 2, core ^ (number % 2)
        group, at = slots[e]
        out = outs[2 * group + number % 2].at[pl.ds(at * upper, upper), :]
        columns = pl.ds(pl.multiple_of(first + target * (main + lanes), 128), main)
        arriving.append(
            [
                pltpu.make_async_copy(
                    w_in_ref.at[SPLIT * e + part, pl.ds(half * upper, upper), columns],
                    held.at[number, :, pl.ds(half * main, main)],
                    sems.at[1 + half, number],
                )
                for half in range(2)
            ]
        )
        leaving.append(pltpu.make_async_copy(held.at[number], out, sems.at[3, number]))
    for copy in rest:
        copy.start()
    for halves in arriving:
        for copy in halves:
            copy.start()
    left = lax.broadcasted_iota(jnp.int32, (upper, lanes), 1) < lanes // 2
    for number, halves in enumerate(arriving):
        e, target = number // 2, core ^ (number % 2)
        if number % 2 == 0:
            rest[e].wait()
        top, bottom = tiles[e, :upper, :], tiles[e, upper:, :]
        low = jnp.where(left, top, halves_turned(bottom))
        high = jnp.where(left, halves_turned(top), bottom)
        held[number, :, 2 * main :] = jnp.where(target == 0, low, high)
        for copy in halves:
            copy.wait()
        leaving[number].start()
    for copy in leaving:
        copy.wait()


def cut_call(w_in, wide, groups):
    units, depth, _ = w_in.shape
    experts = units // SPLIT
    anywhere = pl.BlockSpec(memory_space=pl.ANY)
    blocks = 2 * experts
    return pl.pallas_call(
        functools.partial(cut_kernel, groups),
        in_specs=[anywhere],
        out_specs=[anywhere] * (2 * len(groups)),
        out_shape=[
            jax.ShapeDtypeStruct((len(group) * (depth // 2), wide), jnp.bfloat16)
            for group in groups
            for _ in range(2)
        ],
        scratch_shapes=[
            pltpu.VMEM((blocks, depth // 2, wide), jnp.bfloat16),
            pltpu.VMEM((experts, depth, 128), jnp.bfloat16),
            pltpu.SemaphoreType.DMA((4, blocks)),
        ],
        compiler_params=pltpu.CompilerParams(vmem_limit_bytes=60 << 20),
        cost_estimate=pl.CostEstimate(
            flops=0, bytes_accessed=4 * blocks * (depth // 2) * wide, transcendentals=0
        ),
        name="cut",
    )(w_in)


def expert_kernel(expert, sources, offsets, events, own_ref, b_ref, out_w_ref, *refs):
    x_refs, refs = refs[:sources], refs[sources:]
    near_ref, moved_refs, refs = refs[0], refs[1:5], refs[5 + events :]
    keep_ref, keep_far_ref, send_ref, *refs = refs
    x_pairs, x_held, weight, rest, bias, out_weight, total, sems = refs
    here, part, core = where_am_i()
    depth = own_ref.shape[1]
    columns, width = out_w_ref.shape[1:]
    upper, lanes = rest.shape[2:]
    slab = weight.shape[2]
    skip = slab - columns
    wide = 2 * columns
    main = slab - lanes
    chip_first = pl.multiple_of((here >> 1) * wide + core * (wide - slab), 128)
    half_rows = x_held.shape[0] // 2
    per = x_pairs.shape[1] // 2

    def rows(device, offset, size):
        return pl.ds(pl.multiple_of(device * depth + offset, 16), size)

    made = [[] for _ in range(SPLIT)]
    for number in range(SPLIT):
        unit = SPLIT * expert + (number ^ part)

        def add(source, target, number=number):
            copy = pltpu.make_async_copy(source, target, sems.at[number, len(made[number])])
            made[number].append(copy)

        for ref, device in ((own_ref, here), (near_ref, here ^ 1)):
            add(
                ref.at[unit, :, pl.ds(chip_first, slab)],
                weight.at[number, rows(device, 0, depth), :],
            )
        for at in range(2):
            moved = moved_refs[2 * number + at]
            moved_rows = pl.ds(offsets[2 * number + at], upper)
            for half in range(2):
                add(
                    moved.at[moved_rows, pl.ds(half * main, main)],
                    weight.at[
                        number,
                        rows(here ^ (2 + at), half * upper, upper),
                        pl.ds(pl.multiple_of(core * lanes, 128), main),
                    ],
                )
            add(moved.at[moved_rows, pl.ds(2 * main, lanes)], rest.at[number, at])
        add(b_ref.at[unit], bias.at[number])
        add(
            out_w_ref.at[unit],
            out_weight.at[number, pl.ds(pl.multiple_of(core * skip, 16), columns), :],
        )

    spare_sem = sems.shape[1] - sources
    x_copies = [
        pltpu.make_async_copy(
            x_ref.at[pl.ds(2 * per * (expert // 2), 2 * per), :],
            x_pairs.at[at],
            sems.at[0, spare_sem + at],
        )
        for at, x_ref in enumerate(x_refs)
    ]
    for copy in x_copies + made[0] + made[1]:
        copy.start()
    for number in range(SPLIT):
        spare = pl.ds(pl.multiple_of((1 - core) * columns, 16), skip)
        out_weight[number, spare, :] = jnp.zeros((skip, width), out_weight.dtype)
    for at, copy in enumerate(x_copies):
        copy.wait()
        pair = x_pairs[at].astype(jnp.float32)
        own_rows = pair[per * (expert % 2) : per * (expert % 2 + 1), :]
        total[per * at : per * (at + 1), :] = own_rows
    x_held[...] = total[...].astype(jnp.bfloat16)

    for number in range(SPLIT):
        for copy in made[number][:-1]:
            copy.wait()
        for at in range(2):
            tile = rest[number, at]
            turned = halves_turned(tile)
            for half in range(2):
                at_rows = rows(here ^ (2 + at), half * upper, upper)
                value = jnp.where(core == half, tile, turned)
                tail = pl.ds(pl.multiple_of((1 - core) * main, 128), lanes)
                weight[number, at_rows, tail] = value
        pre = jnp.dot(x_held[...], weight[number], preferred_element_type=jnp.float32)
        hidden = jax.nn.gelu(pre + bias[number], approximate=True).astype(jnp.bfloat16)
        made[number][-1].wait()
        piece = jnp.dot(hidden, out_weight[number], preferred_element_type=jnp.float32)
        total[...] = piece if number == 0 else total[...] + piece

    members = half_rows // (2 * CAP)
    for member in range(members):
        at = 2 * CAP * member
        keep_ref[CAP * member : CAP * (member + 1), :] = total[at : at + CAP, :]
        keep_far_ref[CAP * member : CAP * (member + 1), :] = total[at + CAP : at + 2 * CAP, :]
    given = [
        total[at : at + CAP, :]
        for image in range(2)
        for at in range(half_rows + CAP * image, 2 * half_rows, 2 * CAP)
    ]
    for number, rows_of in enumerate(given):
        total[CAP * number : CAP * (number + 1), :] = rows_of
    send_ref[...] = total[:half_rows, :].astype(jnp.bfloat16)


def expert_call(expert, xs, own, b, w_out, near, moved, events):
    width = w_out.shape[2]
    per = 2 * CAP
    half_rows = per * len(xs) // 2
    depth = own.shape[1]
    columns = w_out.shape[1]
    slab = b.shape[2]
    anywhere = pl.BlockSpec(memory_space=pl.ANY)

    return pl.pallas_call(
        functools.partial(
            expert_kernel, expert, len(xs), [offset for _, offset in moved], len(events)
        ),
        in_specs=[anywhere] * (4 + len(xs) + len(moved) + len(events)),
        out_specs=[pl.BlockSpec(memory_space=pltpu.VMEM)] * 3,
        scratch_shapes=[
            pltpu.VMEM((len(xs), 2 * per, width), jnp.bfloat16),
            pltpu.VMEM((2 * half_rows, width), jnp.bfloat16),
            pltpu.VMEM((SPLIT, width, slab), jnp.bfloat16),
            pltpu.VMEM((SPLIT, 2, depth // 2, 128), jnp.bfloat16),
            pltpu.VMEM((SPLIT, 1, slab), jnp.float32),
            pltpu.VMEM((SPLIT, slab, width), jnp.bfloat16),
            pltpu.VMEM((2 * half_rows, width), jnp.float32),
            pltpu.SemaphoreType.DMA((SPLIT, 10 + len(xs))),
        ],
        out_shape=[
            jax.ShapeDtypeStruct((half_rows // 2, width), jnp.float32),
            jax.ShapeDtypeStruct((half_rows // 2, width), jnp.float32),
            jax.ShapeDtypeStruct((half_rows, width), jnp.bfloat16),
        ],
        compiler_params=pltpu.CompilerParams(vmem_limit_bytes=46 << 20),
        cost_estimate=pl.CostEstimate(
            flops=2 * SPLIT * 2 * 2 * half_rows * width * columns,
            bytes_accessed=3 * (2 * SPLIT * 2 * width * columns + 16 * half_rows * width),
            transcendentals=SPLIT * 2 * half_rows * columns,
        ),
        name="expert",
    )(own, b, w_out, *xs, near, *[held for held, _ in moved], *events)


def combine_kernel(experts, group, last, route_ref, *refs):
    refs, held = refs[:-1], refs[-1]
    refs, out_ref = refs[:-1], refs[-1]
    before_ref = None
    if last:
        (before_ref, tokens_ref, settings_ref), refs = refs[:3], refs[3:]
    count = route_ref.shape[0]
    members = len(refs)
    size = len(group) * CAP
    for at, reply in enumerate(refs):
        held[at * size : (at + 1) * size, :] = reply[...].astype(jnp.float32)
    rows = held[...].astype(jnp.bfloat16)
    place = lax.broadcasted_iota(jnp.int32, (count, members * size), 1).astype(jnp.float32)
    row = lax.axis_index("ep")
    branch = before_ref[...] if last else None
    for k in range(2):
        expert, slot = route_ref[:, k : k + 1], route_ref[:, 2 + k : 3 + k]
        at = jnp.full_like(expert, -1.0)
        for ring in range(members):
            first = (row ^ ring) * experts + group[0]
            local = expert - first.astype(jnp.float32)
            inside = (local >= 0) & (local < len(group))
            at = jnp.where(inside, ring * size + local * CAP + slot, at)
        select = jnp.where(place == at, 1.0, 0.0).astype(jnp.bfloat16)
        term = route_ref[:, 4 + k : 5 + k] * jnp.dot(
            select, rows, preferred_element_type=jnp.float32
        )
        branch = term if branch is None else branch + term
    if last:
        tokens = tokens_ref[0].astype(jnp.float32)
        out_ref[0] = (tokens + settings_ref[2:3, :] * branch).astype(out_ref.dtype)
    else:
        out_ref[...] = branch


def combine_call(experts, group, route, replies, final=None):
    width = replies[0].shape[1]
    out = jax.ShapeDtypeStruct((route.shape[0], width), jnp.float32)
    if final:
        out = jax.ShapeDtypeStruct(final[1].shape, final[1].dtype)
    return pl.pallas_call(
        functools.partial(combine_kernel, experts, group, bool(final)),
        out_shape=out,
        scratch_shapes=[pltpu.VMEM((len(replies) * len(group) * CAP, width), jnp.float32)],
        name="combine",
    )(route, *(final or ()), *replies)


def recut_weights(hidden_states, expert_ids, modulation, router_weight, w_in, b_in, w_out):
    units, depth, _ = w_in.shape
    columns = w_out.shape[1]
    wide = 2 * columns
    experts = units // SPLIT
    members = lax.axis_size("ep")
    here = lax.axis_index("fs")
    core, chip = here & 1, here >> 1
    settings = modulation[0]

    def over(held, *events):
        return crossed(after(held, *events), "fs", 1)

    def beside(held, *events):
        return crossed(after(held, *events), "parts", 1)

    slab = -(-columns // 128) * 128
    own_b = lax.dynamic_slice(
        b_in, (0, chip * wide + core * (wide - slab)), (units, slab)
    )[:, None, :]
    place = np.arange(experts * 2 * CAP)
    image = place // CAP % 2
    wanted = np.where(
        image[:, None] == np.arange(2), (place // (2 * CAP) * CAP + place % CAP)[:, None], -np.inf
    ).astype(np.float32)

    ids = expert_ids[0].T.astype(jnp.float32)
    block = prepare_call(hidden_states, ids, settings)
    gate = after(here, block)
    near = over(w_in)
    opposite = crossed(after(block, gate), "fs", 2)
    upper = depth // 2
    fetched = ((0,), tuple(range(1, experts - 1)), (experts - 1,))
    cuts = cut_call(after(w_in, gate), wide, fetched)

    def fetch(number, *events):
        return crossed(after(cuts[number], *events), "fs", 2 + number % 2)

    def exchange(number, gate):
        size = len(fetched[number // 2])
        blocks = [far[number][at * upper : (at + 1) * upper] for at in range(size)]
        return [beside(held, gate) for held in blocks]

    def run(expert, *events):
        group = [expert in held for held in fetched].index(True)
        at = fetched[group].index(expert)
        moved = [(far[2 * group + k], at * upper) for k in range(2)]
        moved += [(other[2 * group + k][at], 0) for k in range(2)]
        return expert_call(expert, arrived + across, w_in, own_b, w_out, near, moved, events)

    far, other, outs = [fetch(0), fetch(1)], [], []
    opposite, near = lax.optimization_barrier((opposite, near))
    sending = dispatch_call(jnp.asarray(wanted), [block, opposite], members)
    arrived = [sending[0], crossed(sending[1], "ep", 1), crossed(sending[2], "ep", 2)]
    route = route_call(block, router_weight)
    far.append(fetch(2, opposite))
    gate = after(gate, far[0], far[1], near)

    far.append(fetch(3, gate))
    other += [exchange(0, gate), exchange(1, gate)]
    gate = after(gate, far[2], *other[0], *other[1], arrived[1], arrived[2])

    far.append(fetch(4, gate))
    other.append(exchange(2, gate))
    arrived.append(crossed(after(sending[3], gate, route, own_b), "ep", 3))
    gate = after(gate, far[3], *other[2])

    far.append(fetch(5, gate))
    other.append(exchange(3, gate))
    gate = after(gate, far[4], arrived[3])

    other.append(exchange(4, gate))
    across = [over(held, gate) for held in arrived]
    outs.append(run(0))
    gate = after(gate, far[5], *other[3])
    other.append(exchange(5, gate))
    half_rows = members * CAP

    def give(expert):
        held = outs[expert][1] + sent[expert][half_rows:].astype(jnp.float32)
        return crossed(held.astype(jnp.bfloat16), "fs", 2)

    sent = [over(outs[0][2])]
    outs.append(run(1, outs[0][0], far[5], other[3][1]))
    sent.append(over(outs[1][2]))
    given = [give(0), give(1)]
    outs.append(run(2, *sent))
    sent.append(over(outs[2][2]))
    given.append(give(2))
    outs.append(run(3, *given[:2]))
    sent.append(over(outs[3][2]))
    given.append(give(3))

    branch = None
    for group in (tuple(range(experts // 2)), tuple(range(experts // 2, experts))):
        wholes = []
        for e in group:
            half = outs[e][0] + sent[e][:half_rows].astype(jnp.float32)
            wholes.append((half + given[e].astype(jnp.float32)).astype(jnp.bfloat16))
        replies = []
        for d in range(members):
            reply = jnp.concatenate([held[d * CAP : (d + 1) * CAP] for held in wholes])
            replies.append(crossed(after(reply, sent[3]), "ep", d) if d else reply)
        if not group[0]:
            branch = combine_call(experts, group, route, replies)
        else:
            final = (branch, hidden_states, settings)
            branch = combine_call(experts, group, route, replies, final)
    return branch


def local(*arrays):
    w_in = arrays[4]
    recut = lax.axis_size("fs") == lax.axis_size("ep") == 4 and lax.axis_size("parts") == 2
    recut = recut and w_in.shape[0] == 4 * SPLIT and arrays[6].shape[1] % 128 == 64
    return (recut_weights if recut else gathered_weights)(*arrays)


def solution(mesh):
    placed = (
        P(("parts", "fs"), "ep", None),
        P(("parts", "fs"), "ep", None),
        P(("parts", "fs"), None, None),
        P(),
        P("ep", "fs", None),
        P("ep", None),
        P("ep", "fs", None),
    )
    return jax.shard_map(
        local, mesh=mesh, in_specs=placed, out_specs=P(("parts", "fs"), "ep", None), check_vma=False
    )
```
